32 devices in a mesh: lat: 8 (over y, x, core), freq: 4 (over z).
Axes of the slice: x: 2, y: 2, z: 4, core: 2. Of those that a mesh axis runs over, the one named last changes fastest.
Arguments:
- gravity: float32 [128, 21600], P('lat', 'freq'), may hold values from -6 to 6
- coef: bfloat16 [2176, 2, 2176], P(('lat', 'freq')), may hold values from -0.125 to 0.125
- legendre: bfloat16 [2176, 2176, 128], P(('lat', 'freq')), may hold values from -6 to 6
- order_table: int32 [2176], replicated, may hold values from 0 to 2175, as said below
- band_rows: int32 [128], P('lat'), may hold values from 0 to 2399, as said below
- kernel: bfloat16 [255, 10800], P(None, 'freq'), may hold values from -0.5 to 0.5
Outputs:
- geoid: float32 [128, 21600], P('lat', 'freq')
The draws below stay inside these ranges and needn't reach their ends.
Inputs may be any that keep to these rules, and one draw needn't show every extreme that they name: `order_table`: A permutation of the orders 0 to 2175; the slot s lies in the block of slots s // 68, and its order m has m % 4 == (s // 68) % 4. `band_rows`: strictly increasing; the first row is parallel 0 and the last is parallel 2400 - 1.
All inputs are finite; a program needn't handle non-finite values.
Results may differ from the reference program's by a relative error of at most 0.0032.
Values may be sent and summed in bfloat16 or wider, within the bound.
A program may use at most 128 MiB of HBM per device.

```python
import jax
import jax.numpy as jnp
from jax import lax

L = 21600
K = 10800
NORD = 2176
NDEG = 2176
R = 16
PARALLELS = 2400
NBLK = 8
NBAND = 4
RT = 128
OPD = 68
KB = 2700


def group_permutation(subkey):
    return jax.random.permutation(subkey, NORD // NBAND)


def draw_order_table(key, part):
    keys_all = jax.random.split(jax.random.fold_in(key, 11), NBAND)
    perms = jax.vmap(group_permutation)(keys_all)
    slots = jnp.arange(NORD, dtype=jnp.int32)
    block = slots // OPD
    lat_index = block // NBAND
    band = block % NBAND
    within = slots % OPD
    return (perms[band, lat_index * OPD + within] * NBAND + band).astype(jnp.int32)


def draw_band_rows(key, part):
    inner = jax.random.permutation(jax.random.fold_in(key, 17), PARALLELS - 2)[:RT - 2] + 1
    chosen = jnp.sort(inner).astype(jnp.int32)
    first = jnp.zeros((1,), jnp.int32)
    last = jnp.full((1,), PARALLELS - 1, jnp.int32)
    return jnp.concatenate([first, chosen, last])


def steps_of(key, shape, cuts, least, largest):
    level, own = 1.0, jax.random.fold_in(key, 6)
    for dim, blocks in cuts:
        heights = jnp.exp(jax.random.uniform(jax.random.fold_in(own, dim), (blocks,), jnp.float32, least / len(cuts), largest / len(cuts)))
        level = level * jnp.repeat(heights, shape[dim] // blocks).reshape([-1 if axis == dim else 1 for axis in range(len(shape))])
    return level


def scatter_about(key, shape, scale, most, pieces=(), held_as=jnp.bfloat16):
    array = scale * jax.random.normal(key, shape, jnp.float32)
    if pieces:
        array = array * steps_of(key, shape, pieces, -0.22, 0.18)
    return jnp.clip(array, -most, most).astype(held_as)


def setup_inputs(seed: int = 0) -> dict:
    arg_keys = jax.random.split(jax.random.key(seed), 7)
    return {
        "gravity": scatter_about(arg_keys[0], (RT, L), 1.0, 6.0, ((0, 8), (1, 4)), jnp.float32),
        "coef": scatter_about(arg_keys[1], (NORD, 2, NDEG), NDEG ** -0.5, 0.125, ((0, 32),)),
        "legendre": scatter_about(arg_keys[2], (NORD, NDEG, RT), 1.0, 6.0, ((0, 32),)),
        "order_table": draw_order_table(jax.random.fold_in(arg_keys[6], 71), 0),
        "band_rows": draw_band_rows(jax.random.fold_in(arg_keys[6], 71), 0),
        "kernel": scatter_about(arg_keys[5], (2 * RT - 1, K), RT ** -0.5, 0.5, ((1, 4),)),
    }


def reference(gravity, coef, legendre, order_table, band_rows, kernel):
    scale = (2.0 / L) ** 0.5
    spectrum = jnp.fft.fft(gravity, axis=1)[:, :K] * scale
    synth = jnp.einsum('ocn,onq->ocq', coef.astype(jnp.float32), legendre.astype(jnp.float32), precision=lax.Precision.HIGHEST)
    synth = synth.astype(jnp.bfloat16).astype(jnp.float32)
    model_re = jnp.zeros((RT, K), jnp.float32).at[:, order_table].set(synth[:, 0, :].T)
    model_im = jnp.zeros((RT, K), jnp.float32).at[:, order_table].set(synth[:, 1, :].T)
    weight = jnp.cos((20.0 + band_rows.astype(jnp.float32) / 60.0) * (jnp.pi / 180.0))
    weighted = jnp.stack([spectrum.real - model_re, spectrum.imag - model_im]) * weight[None, :, None]
    weighted = weighted.astype(jnp.bfloat16).astype(jnp.float32)
    kernel_freq = kernel.astype(jnp.float32).reshape(2 * RT - 1, NBAND, KB).transpose(0, 2, 1).reshape(2 * RT - 1, K)

    def one_block(first):
        targets = first + jnp.arange(R, dtype=jnp.int32)
        position = jnp.arange(RT, dtype=jnp.int32)[None, :] - targets[:, None] + RT - 1
        toeplitz = kernel_freq[position]
        return jnp.einsum('pqk,cqk->cpk', toeplitz, weighted, precision=lax.Precision.HIGHEST)

    blocks_out = lax.map(one_block, jnp.arange(NBLK, dtype=jnp.int32) * R)
    stokes = blocks_out.transpose(1, 0, 2, 3).reshape(2, RT, K)
    padded = jnp.pad(stokes[0] + 1j * stokes[1], ((0, 0), (0, L - K)))
    geoid = jnp.fft.ifft(padded, axis=1).real * (L * scale)
    return geoid.astype(jnp.float32)
```

```python
import jax
import jax.numpy as jnp
import numpy as np
from jax import lax
from jax.experimental import pallas as pl
from jax.experimental.pallas import tpu as pltpu
from jax.sharding import PartitionSpec as P

L = 21600
PA = 144
PB = 150
PH = 75


highest = lax.Precision.HIGHEST


def angle_table(first, second, period):
    phase = first * second % period
    return phase.astype(jnp.float32) * (2.0 * np.pi / period)


def forward_bands(grid, first_start, bands):
    rows = grid.shape[0]
    count_one = grid.shape[1]
    first_index = first_start + jnp.arange(count_one, dtype=jnp.int32)
    freq_one = jnp.arange(PA, dtype=jnp.int32)
    theta_one = angle_table(first_index[:, None], freq_one[None, :], PA)
    section_re = jnp.einsum("rab,ak->rbk", grid, jnp.cos(theta_one), precision=highest)
    section_im = -jnp.einsum("rab,ak->rbk", grid, jnp.sin(theta_one), precision=highest)
    second_index = jnp.arange(PB, dtype=jnp.int32)
    twist = angle_table(second_index[:, None], freq_one[None, :], L)
    twist_cos = jnp.cos(twist)
    twist_sin = jnp.sin(twist)
    turned_re = section_re * twist_cos + section_im * twist_sin
    turned_im = section_im * twist_cos - section_re * twist_sin
    freq_two = jnp.arange(PH, dtype=jnp.int32)
    theta_two = angle_table(second_index[:, None], freq_two[None, :], PB)
    cos_two = jnp.cos(theta_two)
    sin_two = jnp.sin(theta_two)
    spec_re = jnp.einsum("rbk,bm->rkm", turned_re, cos_two, precision=highest) + jnp.einsum(
        "rbk,bm->rkm", turned_im, sin_two, precision=highest
    )
    spec_im = jnp.einsum("rbk,bm->rkm", turned_im, cos_two, precision=highest) - jnp.einsum(
        "rbk,bm->rkm", turned_re, sin_two, precision=highest
    )
    scale = (2.0 / L) ** 0.5
    stacked = jnp.stack([spec_re, spec_im]) * scale
    span = PA // bands
    stacked = stacked.reshape(2, rows, span, bands, PH).transpose(3, 1, 0, 4, 2)
    return stacked.reshape(bands, rows, 2, PH * span)


def inverse_rows(spectra, band_ids, bands):
    count = spectra.shape[0]
    rows = spectra.shape[1]
    span = PA // bands
    parts = spectra.reshape(count, rows, 2, PH, span)
    part_re = parts[:, :, 0]
    part_im = parts[:, :, 1]
    freq_two = jnp.arange(PH, dtype=jnp.int32)
    second_index = jnp.arange(PB, dtype=jnp.int32)
    theta_two = angle_table(freq_two[:, None], second_index[None, :], PB)
    cos_two = jnp.cos(theta_two)
    sin_two = jnp.sin(theta_two)
    middle_re = jnp.einsum("brms,mn->brsn", part_re, cos_two, precision=highest) - jnp.einsum(
        "brms,mn->brsn", part_im, sin_two, precision=highest
    )
    middle_im = jnp.einsum("brms,mn->brsn", part_im, cos_two, precision=highest) + jnp.einsum(
        "brms,mn->brsn", part_re, sin_two, precision=highest
    )
    freq_one = jnp.arange(span, dtype=jnp.int32)[None, :] * bands + band_ids[:, None]
    twist = angle_table(freq_one[:, :, None], second_index[None, None, :], L)
    twist_cos = jnp.cos(twist)[:, None]
    twist_sin = jnp.sin(twist)[:, None]
    turned_re = middle_re * twist_cos - middle_im * twist_sin
    turned_im = middle_re * twist_sin + middle_im * twist_cos
    first_index = jnp.arange(PA, dtype=jnp.int32)
    theta_one = angle_table(freq_one[:, :, None], first_index[None, None, :], PA)
    grid = jnp.einsum(
        "brsn,bsa->ran", turned_re, jnp.cos(theta_one), precision=highest
    ) - jnp.einsum("brsn,bsa->ran", turned_im, jnp.sin(theta_one), precision=highest)
    return grid * (2.0 / L) ** 0.5


def general_device(gravity, coef, legendre, order_table, band_rows, kernel):
    bands = lax.axis_size("freq")
    blocks = lax.axis_size("lat")
    band_self = lax.axis_index("freq")
    block_self = lax.axis_index("lat")
    rows = gravity.shape[0]
    span = PA // bands
    local_grid = gravity.reshape(rows, span, PB)
    terms = forward_bands(local_grid, band_self * span, bands)
    observed = lax.psum_scatter(terms, "freq", scatter_dimension=0, tiled=True)[0]
    band_width = observed.shape[2]
    synth = jnp.einsum("ocn,onq->ocq", coef, legendre, preferred_element_type=jnp.float32).astype(
        jnp.bfloat16
    )
    routed = lax.all_to_all(synth, "lat", split_axis=2, concat_axis=0, tiled=True)
    per_slot = coef.shape[0]
    slot_ids = (
        (jnp.arange(blocks, dtype=jnp.int32)[:, None] * bands + band_self) * per_slot
        + jnp.arange(per_slot, dtype=jnp.int32)[None, :]
    ).reshape(-1)
    positions = order_table[slot_ids] // bands
    selector = (positions[:, None] == jnp.arange(band_width, dtype=jnp.int32)[None, :]).astype(
        jnp.bfloat16
    )
    model = jnp.einsum("jcr,jt->rct", routed, selector, preferred_element_type=jnp.float32)
    weight = jnp.cos((20.0 + band_rows.astype(jnp.float32) / 60.0) * (np.pi / 180.0))
    weighted = ((observed - model) * weight[:, None, None]).astype(jnp.bfloat16)
    total_rows = rows * blocks
    padded_width = -(-band_width // blocks) * blocks
    padding_cols = padded_width - band_width
    slab_width = padded_width // blocks
    spread = jnp.pad(weighted, ((0, 0), (0, 0), (0, padding_cols)))
    columns = lax.all_to_all(spread, "lat", split_axis=2, concat_axis=0, tiled=True)
    kernel_padded = jnp.pad(kernel, ((0, 0), (0, padding_cols)))
    kernel_own = lax.dynamic_slice_in_dim(kernel_padded, block_self * slab_width, slab_width, 1)
    full_offsets = np.arange(total_rows)[None, :] - np.arange(total_rows)[:, None] + total_rows - 1
    toeplitz_full = kernel_own[full_offsets]
    summed = jnp.einsum("pqk,qck->pck", toeplitz_full, columns, preferred_element_type=jnp.float32)
    returned = lax.all_to_all(summed, "lat", split_axis=0, concat_axis=2, tiled=True)
    stokes = returned[:, :, :band_width]
    grid_terms = inverse_rows(stokes[None], jnp.reshape(band_self, (1,)), bands)
    geoid = lax.psum_scatter(grid_terms, "freq", scatter_dimension=1, tiled=True)
    return geoid.reshape(rows, span * PB)


NA = 45
NC = 120
AP = 48
HALF = 64
CP = 128
SCALE = (2.0 / L) ** 0.5
SHIFT = 2.0**-7


def split_pair(values):
    high = values.astype(jnp.bfloat16)
    low = (values - high.astype(jnp.float32)).astype(jnp.bfloat16)
    return high, low


def numpy_pair(values):
    high = np.asarray(values, np.float32).astype(jnp.bfloat16)
    low = (values - high.astype(np.float64)).astype(jnp.bfloat16)
    return high, low


def tables():
    a = np.arange(NA)
    c = np.arange(NC)
    j1 = np.arange(NA)
    j2 = np.arange(NC // 2)
    first = np.zeros((4, CP, 2 * AP))
    twist = np.zeros((4, 2, HALF, CP))
    for b in range(4):
        theta = 2 * np.pi * (np.outer(4 * j1 + b, a) % (4 * NA)) / (4 * NA)
        first[b, :NA, :NA] = np.cos(theta)
        first[b, :NA, AP : AP + NA] = np.sin(theta)
        first[b, HALF : HALF + NA, :NA] = -np.sin(theta)
        first[b, HALF : HALF + NA, AP : AP + NA] = np.cos(theta)
        phi = 2 * np.pi * (np.outer(4 * j1 + b, c) % L) / L
        twist[b, 0, :NA, :NC] = np.cos(phi)
        twist[b, 1, :NA, :NC] = np.sin(phi)
    second = np.zeros((CP, CP))
    angle = 2 * np.pi * (np.outer(j2, c) % NC) / NC
    second[: NC // 2, :NC] = np.cos(angle)
    second[HALF : HALF + NC // 2, :NC] = np.sin(angle)
    return first, twist, second


def three_cols(values):
    high, low = numpy_pair(values)
    return np.concatenate([high, high, low], axis=-1)


def rows_of_three(values):
    high, low = split_pair(values)
    return jnp.concatenate([high, low, high], axis=0)


def cols_of_three(values):
    high, low = split_pair(values)
    return jnp.concatenate([high, low, high], axis=1)


def lane_sign():
    lane = lax.broadcasted_iota(jnp.int32, (1, CP), 1)
    return jnp.where(lane < HALF, 1.0, -1.0)


def forward_kernel(re_ref, im_ref, model_ref, weight_ref, first_ref, twist_ref, second_ref, out_ref, grid):
    band = lax.axis_index("freq")
    rows = re_ref.shape[0]
    grid[...] = jnp.zeros_like(grid)
    for a in range(NA):
        grid[:, a, :NC] = re_ref[:, a * NC : (a + 1) * NC]
        grid[:, AP + a, :NC] = im_ref[:, a * NC : (a + 1) * NC]
    first = first_ref[band]
    cosine = twist_ref[band, 0]
    sine = twist_ref[band, 1]
    second = second_ref[...]
    sign = lane_sign() * SCALE
    for r in range(rows):
        section = jnp.dot(first, rows_of_three(grid[r]), preferred_element_type=jnp.float32)
        top, bottom = section[:HALF], section[HALF:]
        turned = jnp.concatenate([top * cosine + bottom * sine, bottom * cosine - top * sine], axis=0)
        both = lax.dot_general(
            second, cols_of_three(turned), (((1,), (1,)), ((), ())), preferred_element_type=jnp.float32
        )
        spectrum = both[:HALF] * SCALE + pltpu.roll(both[HALF:], HALF, 1) * sign
        held = model_ref.shape[1]
        weight = weight_ref[r]
        out_ref[r, :held] = (spectrum[:held] - model_ref[r]) * weight
        out_ref[r, held:] = spectrum[held:] * weight


def inverse_kernel(in_ref, first_ref, twist_ref, second_ref, re_ref, own_ref, grid):
    band = lax.axis_index("freq")
    rows = in_ref.shape[0]
    first = first_ref[band]
    cosine = twist_ref[band, 0]
    sine = twist_ref[band, 1]
    second = second_ref[...]
    sign = lane_sign() * SCALE
    for r in range(rows):
        both = jnp.dot(second, rows_of_three(in_ref[r]), preferred_element_type=jnp.float32)
        middle = both[:CP] * SCALE - pltpu.roll(both[CP:], HALF, 1) * sign
        turned = middle * cosine + pltpu.roll(middle, HALF, 1) * sine
        grid[r] = lax.dot_general(
            first, cols_of_three(turned), (((1,), (1,)), ((), ())), preferred_element_type=jnp.float32
        )
    even = band % 2 == 0
    for a in range(NA):
        real = grid[:, a, :NC]
        re_ref[:, a * NC : (a + 1) * NC] = real
        own_ref[:, a * NC : (a + 1) * NC] = jnp.where(even, real, grid[:, AP + a, :NC])


def stokes_kernel(kernel_ref, weighted_ref, out_ref):
    total = weighted_ref.shape[0]
    pb, qb = 16, 8

    def p_step(i, carry):
        p0 = i * pb

        def q_step(j, acc):
            q0 = j * qb
            base = q0 - p0 + total - 1 - (pb - 1)
            window = [kernel_ref[base + d] for d in range(pb + qb - 1)]
            values = [weighted_ref[q0 + q].astype(jnp.float32) for q in range(qb)]
            acc = list(acc)
            for p in range(pb):
                for q in range(qb):
                    acc[p] = acc[p] + window[q - p + pb - 1] * values[q]
            return tuple(acc)

        zero = jnp.zeros(out_ref.shape[1:], jnp.float32)
        acc = lax.fori_loop(0, total // qb, q_step, (zero,) * pb)
        for p in range(pb):
            out_ref[p0 + p] = acc[p]
        return carry

    lax.fori_loop(0, total // pb, p_step, 0)


def swap(values, distance):
    return lax.ppermute(values, "freq", [(f, f ^ distance) for f in range(4)])


def pick(values, band):
    return jnp.asarray(values, jnp.float32)[band]


def band_device(gravity, coef, legendre, order_table, band_rows, kernel):
    band = lax.axis_index("freq")
    blocks = lax.axis_size("lat")
    block = lax.axis_index("lat")
    rows = gravity.shape[0]
    total = rows * blocks
    slots = coef.shape[0]
    deep = HALF // blocks
    first, twist, second = tables()
    vmem = pl.BlockSpec(memory_space=pltpu.VMEM)
    params = pltpu.CompilerParams(vmem_limit_bytes=48 * 2**20)

    even = band % 2 == 0
    lower = band < 2
    short = gravity.astype(jnp.float16)
    across = swap(short, 2).astype(jnp.float32)
    added = gravity + across
    taken = jnp.where(lower, gravity - across, across - gravity)
    beside = swap(jnp.where(even, taken, added).astype(jnp.float16), 1).astype(jnp.float32)
    h_re = jnp.where(even, added + jnp.where(lower, beside, -beside), beside)
    h_im = jnp.where(even, 0.0, jnp.where(lower, -taken, taken))

    synth = jnp.einsum("ocn,onq->ocq", coef, legendre, preferred_element_type=jnp.float32).astype(jnp.bfloat16)
    routed = lax.all_to_all(synth, "lat", split_axis=2, concat_axis=0, tiled=True)
    held = -(-(-(-order_table.shape[0] // 4) // NA) // 8) * 8
    mine = lax.dynamic_index_in_dim(order_table.reshape(blocks, 4, slots), band, 1, keepdims=False)
    place = mine.reshape(-1) // 4
    lane = place // NA * HALF + place % NA
    selector = (lane[:, None] == jnp.arange(held * HALF, dtype=jnp.int32)[None, :]).astype(jnp.bfloat16)
    model = jnp.einsum("jcr,jt->rct", routed, selector, preferred_element_type=jnp.float32)
    model = model.reshape(rows, 2, held, HALF).transpose(0, 2, 1, 3).reshape(rows, held, 2 * HALF)
    weight = jnp.cos((20.0 + band_rows.astype(jnp.float32) / 60.0) * (np.pi / 180.0))
    weight = jnp.broadcast_to(weight[:, None, None], (rows, 1, CP))

    forward_twist = twist.astype(np.float32)
    weighted = pl.pallas_call(
        forward_kernel,
        out_shape=jax.ShapeDtypeStruct((rows, HALF, CP), jnp.float32),
        in_specs=[vmem] * 7,
        out_specs=vmem,
        scratch_shapes=[pltpu.VMEM((rows, 2 * AP, CP), jnp.float32)],
        compiler_params=params,
        name="longitude_forward",
    )(h_re, h_im, model, weight, three_cols(first), forward_twist, three_cols(second))
    weighted = weighted.astype(jnp.bfloat16).reshape(rows, blocks, deep, CP)
    columns = lax.all_to_all(weighted, "lat", split_axis=1, concat_axis=0, tiled=True).reshape(total, deep, CP)

    width = deep * NA
    padded = jnp.pad(kernel, ((0, 0), (0, width * blocks - kernel.shape[1])))
    own = lax.dynamic_slice_in_dim(padded, block * width, width, 1).reshape(2 * total - 1, deep, NA)
    own = jnp.pad(own, ((0, 0), (0, 0), (0, HALF - NA)))
    own = jnp.concatenate([own, own], axis=2).astype(jnp.float32)
    summed = pl.pallas_call(
        stokes_kernel,
        out_shape=jax.ShapeDtypeStruct((total, deep, CP), jnp.float32),
        in_specs=[vmem] * 2,
        out_specs=vmem,
        compiler_params=params,
        name="stokes_rows",
    )(own, columns)
    returned = lax.all_to_all(summed.reshape(total, 1, deep, CP), "lat", split_axis=0, concat_axis=1, tiled=True)

    back_second = three_cols(np.concatenate([second[:HALF].T, second[HALF:].T], axis=0))
    turn = np.concatenate([twist[:, 0], twist[:, 0]], axis=1), np.concatenate([-twist[:, 1], twist[:, 1]], axis=1)
    back_twist = np.stack([turn[0].transpose(0, 2, 1), turn[1].transpose(0, 2, 1)], axis=1).astype(np.float32)
    back_first = three_cols(first.transpose(0, 2, 1))
    flat = jax.ShapeDtypeStruct(gravity.shape, jnp.float32)
    real, chosen = pl.pallas_call(
        inverse_kernel,
        out_shape=(flat, flat),
        in_specs=[vmem] * 4,
        out_specs=(vmem, vmem),
        scratch_shapes=[pltpu.VMEM((rows, 2 * AP, CP), jnp.float32)],
        compiler_params=params,
        name="longitude_inverse",
    )(returned.reshape(rows, HALF, CP), back_first, back_twist, back_second)

    beside = swap((real * SHIFT).astype(jnp.float16), 1).astype(jnp.float32) / SHIFT
    keep = pick([1, -1, 1, -1], band) * chosen + pick([1, 1, -1, -1], band) * beside
    give = chosen + pick([-1, 1, 1, -1], band) * beside
    return keep + swap((give * SHIFT).astype(jnp.float16), 2).astype(jnp.float32) / SHIFT


def fits(mesh):
    return mesh.shape["freq"] == 4 and HALF % mesh.shape["lat"] == 0


def solution(mesh):
    return jax.shard_map(
        band_device if fits(mesh) else general_device,
        mesh=mesh,
        in_specs=(
            P("lat", "freq"),
            P(("lat", "freq"), None, None),
            P(("lat", "freq"), None, None),
            P(),
            P("lat"),
            P(None, "freq"),
        ),
        out_specs=P("lat", "freq"),
        check_vma=False,
    )
```

```python
import functools

import jax
import jax.numpy as jnp
import numpy as np
from jax import lax
from jax.experimental import pallas as pl
from jax.experimental.pallas import tpu as pltpu
from jax.sharding import PartitionSpec as P

L = 21600
PA = 144
PB = 150
PH = 75


highest = lax.Precision.HIGHEST


def angle_table(first, second, period):
    phase = first * second % period
    return phase.astype(jnp.float32) * (2.0 * np.pi / period)


def forward_bands(grid, first_start, bands):
    rows = grid.shape[0]
    count_one = grid.shape[1]
    first_index = first_start + jnp.arange(count_one, dtype=jnp.int32)
    freq_one = jnp.arange(PA, dtype=jnp.int32)
    theta_one = angle_table(first_index[:, None], freq_one[None, :], PA)
    section_re = jnp.einsum("rab,ak->rbk", grid, jnp.cos(theta_one), precision=highest)
    section_im = -jnp.einsum("rab,ak->rbk", grid, jnp.sin(theta_one), precision=highest)
    second_index = jnp.arange(PB, dtype=jnp.int32)
    twist = angle_table(second_index[:, None], freq_one[None, :], L)
    twist_cos = jnp.cos(twist)
    twist_sin = jnp.sin(twist)
    turned_re = section_re * twist_cos + section_im * twist_sin
    turned_im = section_im * twist_cos - section_re * twist_sin
    freq_two = jnp.arange(PH, dtype=jnp.int32)
    theta_two = angle_table(second_index[:, None], freq_two[None, :], PB)
    cos_two = jnp.cos(theta_two)
    sin_two = jnp.sin(theta_two)
    spec_re = jnp.einsum("rbk,bm->rkm", turned_re, cos_two, precision=highest) + jnp.einsum(
        "rbk,bm->rkm", turned_im, sin_two, precision=highest
    )
    spec_im = jnp.einsum("rbk,bm->rkm", turned_im, cos_two, precision=highest) - jnp.einsum(
        "rbk,bm->rkm", turned_re, sin_two, precision=highest
    )
    scale = (2.0 / L) ** 0.5
    stacked = jnp.stack([spec_re, spec_im]) * scale
    span = PA // bands
    stacked = stacked.reshape(2, rows, span, bands, PH).transpose(3, 1, 0, 4, 2)
    return stacked.reshape(bands, rows, 2, PH * span)


def inverse_rows(spectra, band_ids, bands):
    count = spectra.shape[0]
    rows = spectra.shape[1]
    span = PA // bands
    parts = spectra.reshape(count, rows, 2, PH, span)
    part_re = parts[:, :, 0]
    part_im = parts[:, :, 1]
    freq_two = jnp.arange(PH, dtype=jnp.int32)
    second_index = jnp.arange(PB, dtype=jnp.int32)
    theta_two = angle_table(freq_two[:, None], second_index[None, :], PB)
    cos_two = jnp.cos(theta_two)
    sin_two = jnp.sin(theta_two)
    middle_re = jnp.einsum("brms,mn->brsn", part_re, cos_two, precision=highest) - jnp.einsum(
        "brms,mn->brsn", part_im, sin_two, precision=highest
    )
    middle_im = jnp.einsum("brms,mn->brsn", part_im, cos_two, precision=highest) + jnp.einsum(
        "brms,mn->brsn", part_re, sin_two, precision=highest
    )
    freq_one = jnp.arange(span, dtype=jnp.int32)[None, :] * bands + band_ids[:, None]
    twist = angle_table(freq_one[:, :, None], second_index[None, None, :], L)
    twist_cos = jnp.cos(twist)[:, None]
    twist_sin = jnp.sin(twist)[:, None]
    turned_re = middle_re * twist_cos - middle_im * twist_sin
    turned_im = middle_re * twist_sin + middle_im * twist_cos
    first_index = jnp.arange(PA, dtype=jnp.int32)
    theta_one = angle_table(freq_one[:, :, None], first_index[None, None, :], PA)
    grid = jnp.einsum(
        "brsn,bsa->ran", turned_re, jnp.cos(theta_one), precision=highest
    ) - jnp.einsum("brsn,bsa->ran", turned_im, jnp.sin(theta_one), precision=highest)
    return grid * (2.0 / L) ** 0.5


def general_device(gravity, coef, legendre, order_table, band_rows, kernel):
    bands = lax.axis_size("freq")
    blocks = lax.axis_size("lat")
    band_self = lax.axis_index("freq")
    block_self = lax.axis_index("lat")
    rows = gravity.shape[0]
    span = PA // bands
    local_grid = gravity.reshape(rows, span, PB)
    terms = forward_bands(local_grid, band_self * span, bands)
    observed = lax.psum_scatter(terms, "freq", scatter_dimension=0, tiled=True)[0]
    band_width = observed.shape[2]
    synth = jnp.einsum("ocn,onq->ocq", coef, legendre, preferred_element_type=jnp.float32).astype(
        jnp.bfloat16
    )
    routed = lax.all_to_all(synth, "lat", split_axis=2, concat_axis=0, tiled=True)
    per_slot = coef.shape[0]
    slot_ids = (
        (jnp.arange(blocks, dtype=jnp.int32)[:, None] * bands + band_self) * per_slot
        + jnp.arange(per_slot, dtype=jnp.int32)[None, :]
    ).reshape(-1)
    positions = order_table[slot_ids] // bands
    selector = (positions[:, None] == jnp.arange(band_width, dtype=jnp.int32)[None, :]).astype(
        jnp.bfloat16
    )
    model = jnp.einsum("jcr,jt->rct", routed, selector, preferred_element_type=jnp.float32)
    weight = jnp.cos((20.0 + band_rows.astype(jnp.float32) / 60.0) * (np.pi / 180.0))
    weighted = ((observed - model) * weight[:, None, None]).astype(jnp.bfloat16)
    total_rows = rows * blocks
    padded_width = -(-band_width // blocks) * blocks
    padding_cols = padded_width - band_width
    slab_width = padded_width // blocks
    spread = jnp.pad(weighted, ((0, 0), (0, 0), (0, padding_cols)))
    columns = lax.all_to_all(spread, "lat", split_axis=2, concat_axis=0, tiled=True)
    kernel_padded = jnp.pad(kernel, ((0, 0), (0, padding_cols)))
    kernel_own = lax.dynamic_slice_in_dim(kernel_padded, block_self * slab_width, slab_width, 1)
    full_offsets = np.arange(total_rows)[None, :] - np.arange(total_rows)[:, None] + total_rows - 1
    toeplitz_full = kernel_own[full_offsets]
    summed = jnp.einsum("pqk,qck->pck", toeplitz_full, columns, preferred_element_type=jnp.float32)
    returned = lax.all_to_all(summed, "lat", split_axis=0, concat_axis=2, tiled=True)
    stokes = returned[:, :, :band_width]
    grid_terms = inverse_rows(stokes[None], jnp.reshape(band_self, (1,)), bands)
    geoid = lax.psum_scatter(grid_terms, "freq", scatter_dimension=1, tiled=True)
    return geoid.reshape(rows, span * PB)


NA = 45
NC = 120
AP = 48
HALF = 64
CP = 128
SCALE = (2.0 / L) ** 0.5
SHIFT = 2.0**-7


def split_pair(values):
    high = values.astype(jnp.bfloat16)
    low = (values - high.astype(jnp.float32)).astype(jnp.bfloat16)
    return high, low


def numpy_pair(values):
    high = np.asarray(values, np.float32).astype(jnp.bfloat16)
    low = (values - high.astype(np.float64)).astype(jnp.bfloat16)
    return high, low


def tables():
    a = np.arange(NA)
    c = np.arange(NC)
    j1 = np.arange(NA)
    j2 = np.arange(NC // 2)
    first = np.zeros((4, CP, 2 * AP))
    twist = np.zeros((4, 2, HALF, CP))
    for b in range(4):
        theta = 2 * np.pi * (np.outer(4 * j1 + b, a) % (4 * NA)) / (4 * NA)
        first[b, :NA, :NA] = np.cos(theta)
        first[b, :NA, AP : AP + NA] = np.sin(theta)
        first[b, HALF : HALF + NA, :NA] = -np.sin(theta)
        first[b, HALF : HALF + NA, AP : AP + NA] = np.cos(theta)
        phi = 2 * np.pi * (np.outer(4 * j1 + b, c) % L) / L
        twist[b, 0, :NA, :NC] = np.cos(phi)
        twist[b, 1, :NA, :NC] = np.sin(phi)
    second = np.zeros((CP, CP))
    angle = 2 * np.pi * (np.outer(j2, c) % NC) / NC
    second[: NC // 2, :NC] = np.cos(angle)
    second[HALF : HALF + NC // 2, :NC] = np.sin(angle)
    return first, twist, second


def three_cols(values):
    high, low = numpy_pair(values)
    return np.concatenate([high, high, low], axis=-1)


def rows_of_three(values):
    high, low = split_pair(values)
    return jnp.concatenate([high, low, high], axis=0)


def cols_of_three(values):
    high, low = split_pair(values)
    return jnp.concatenate([high, low, high], axis=1)


def lane_sign():
    lane = lax.broadcasted_iota(jnp.int32, (1, CP), 1)
    return jnp.where(lane < HALF, 1.0, -1.0)


def forward_kernel(re_ref, im_ref, model_ref, weight_ref, first_ref, twist_ref, second_ref, out_ref, grid, parts):
    band = lax.axis_index("freq")
    rows = re_ref.shape[0]
    blocks = out_ref.shape[0]
    deep = HALF // blocks
    grid[...] = jnp.zeros_like(grid)
    for a in range(NA):
        grid[:, a, :NC] = re_ref[:, a * NC : (a + 1) * NC]
        grid[:, AP + a, :NC] = im_ref[:, a * NC : (a + 1) * NC]
    first = first_ref[band]
    cosine = twist_ref[band, 0]
    sine = twist_ref[band, 1]
    second = second_ref[...]
    sign = lane_sign() * SCALE
    for r in range(rows):
        section = jnp.dot(first, rows_of_three(grid[r]), preferred_element_type=jnp.float32)
        top, bottom = section[:HALF], section[HALF:]
        turned = jnp.concatenate([top * cosine + bottom * sine, bottom * cosine - top * sine], axis=0)
        both = lax.dot_general(
            second, cols_of_three(turned), (((1,), (1,)), ((), ())), preferred_element_type=jnp.float32
        )
        spectrum = both[:HALF] * SCALE + pltpu.roll(both[HALF:], HALF, 1) * sign
        held = model_ref.shape[1]
        weight = weight_ref[r]
        residual = jnp.concatenate([spectrum[:held] - model_ref[r], spectrum[held:]], axis=0) * weight
        parts[:, r * deep : (r + 1) * deep] = residual.reshape(blocks, deep, CP)
    out_ref[...] = parts[...].astype(out_ref.dtype)


def inverse_kernel(start, in_ref, first_ref, twist_ref, second_ref, re_ref, own_ref, grid, wide):
    band = lax.axis_index("freq")
    rows = re_ref.shape[0]
    blocks = in_ref.shape[0]
    deep = HALF // blocks
    first = first_ref[band]
    cosine = twist_ref[band, 0]
    sine = twist_ref[band, 1]
    second = second_ref[...]
    sign = lane_sign() * SCALE
    wide[...] = in_ref[:, start * deep : (start + rows) * deep].astype(jnp.float32)
    for r in range(rows):
        sums = wide[:, r * deep : (r + 1) * deep].reshape(HALF, CP).astype(jnp.bfloat16)
        both = jnp.dot(second, jnp.concatenate([sums, sums], axis=0), preferred_element_type=jnp.float32)
        middle = both[:CP] * SCALE - pltpu.roll(both[CP:], HALF, 1) * sign
        turned = middle * cosine + pltpu.roll(middle, HALF, 1) * sine
        grid[r] = lax.dot_general(
            first, cols_of_three(turned), (((1,), (1,)), ((), ())), preferred_element_type=jnp.float32
        )
    even = band % 2 == 0
    for a in range(NA):
        real = grid[:, a, :NC]
        re_ref[:, a * NC : (a + 1) * NC] = real
        own_ref[:, a * NC : (a + 1) * NC] = jnp.where(even, real, grid[:, AP + a, :NC])


def stokes_kernel(kernel_ref, weighted_ref, out_ref, values, sums):
    blocks = weighted_ref.shape[0]
    total = values.shape[0]
    deep = values.shape[1]
    share = total // blocks
    pb, qb = 16, 8
    for source in range(blocks):
        values[source * share : (source + 1) * share] = (
            weighted_ref[source].astype(jnp.float32).reshape(share, deep, CP)
        )

    def p_step(i, carry):
        p0 = i * pb

        def q_step(j, acc):
            q0 = j * qb
            base = q0 - p0 + total - 1 - (pb - 1)
            window = [kernel_ref[base + d] for d in range(pb + qb - 1)]
            terms = [values[q0 + q] for q in range(qb)]
            acc = list(acc)
            for p in range(pb):
                for q in range(qb):
                    acc[p] = acc[p] + window[q - p + pb - 1] * terms[q]
            return tuple(acc)

        zero = jnp.zeros(values.shape[1:], jnp.float32)
        acc = lax.fori_loop(0, total // qb, q_step, (zero,) * pb)
        for p in range(pb):
            sums[p0 + p] = acc[p]
        return carry

    lax.fori_loop(0, total // pb, p_step, 0)
    for target in range(blocks):
        block = sums[target * share : (target + 1) * share].reshape(share * deep, CP)
        out_ref[target] = block.astype(out_ref.dtype)


def exchange_kernel(src, dst, send, recv, near):
    me = lax.axis_index("lat")
    count = src.shape[0]
    peers = [lax.rem(me + d, count) for d in range(1, count)]
    barrier = pltpu.get_barrier_semaphore()
    for peer in peers:
        pl.semaphore_signal(barrier, inc=1, device_id={"lat": peer}, device_id_type=pl.DeviceIdType.MESH)
    pl.semaphore_wait(barrier, count - 1)
    copies = []
    for d, peer in enumerate(peers):
        copy = pltpu.make_async_remote_copy(
            src_ref=src.at[peer],
            dst_ref=dst.at[me],
            send_sem=send.at[d],
            recv_sem=recv.at[d],
            device_id={"lat": peer},
            device_id_type=pl.DeviceIdType.MESH,
        )
        copy.start()
        copies.append(copy)
    own = pltpu.make_async_copy(src.at[me], dst.at[me], near)
    own.start()
    own.wait()
    for copy in copies:
        copy.wait()


def exchange(values, number, name):
    count = values.shape[0]
    vmem = pl.BlockSpec(memory_space=pltpu.VMEM)
    return pl.pallas_call(
        exchange_kernel,
        out_shape=jax.ShapeDtypeStruct(values.shape, values.dtype),
        in_specs=[vmem],
        out_specs=vmem,
        scratch_shapes=[
            pltpu.SemaphoreType.DMA((count - 1,)),
            pltpu.SemaphoreType.DMA((count - 1,)),
            pltpu.SemaphoreType.DMA,
        ],
        compiler_params=pltpu.CompilerParams(
            collective_id=number, has_side_effects=True, vmem_limit_bytes=32 * 2**20
        ),
        name=name,
    )(values)


def swap(values, distance):
    return lax.ppermute(values, "freq", [(f, f ^ distance) for f in range(4)])


def band_device(gravity, coef, legendre, order_table, band_rows, kernel):
    band = lax.axis_index("freq")
    blocks = lax.axis_size("lat")
    block = lax.axis_index("lat")
    rows = gravity.shape[0]
    total = rows * blocks
    slots = coef.shape[0]
    deep = HALF // blocks
    first, twist, second = tables()
    vmem = pl.BlockSpec(memory_space=pltpu.VMEM)
    params = pltpu.CompilerParams(vmem_limit_bytes=48 * 2**20)

    even = band % 2 == 0
    lower = band < 2
    short = gravity.astype(jnp.float16)
    across = swap(short, 2).astype(jnp.float32)
    added = gravity + across
    taken = jnp.where(lower, gravity - across, across - gravity)
    beside = swap(jnp.where(even, taken, added).astype(jnp.float16), 1).astype(jnp.float32)
    h_re = jnp.where(even, added + jnp.where(lower, beside, -beside), beside)
    h_im = jnp.where(even, 0.0, jnp.where(lower, -taken, taken))

    synth = jnp.einsum("ocn,onq->ocq", coef, legendre, preferred_element_type=jnp.float32).astype(jnp.bfloat16)
    synth = synth.reshape(slots, 2, blocks, rows).transpose(2, 3, 1, 0).reshape(blocks, rows * 2, slots)
    synth = jnp.pad(synth, ((0, 0), (0, 0), (0, CP - slots)))
    routed = exchange(synth, 0, "route_synth")
    held = -(-(-(-order_table.shape[0] // 4) // NA) // 8) * 8
    mine = lax.dynamic_index_in_dim(order_table.reshape(blocks, 4, slots), band, 1, keepdims=False)
    place = mine // 4
    lane = jnp.pad(place // NA * HALF + place % NA, ((0, 0), (0, CP - slots)), constant_values=-1)
    selector = (lane[:, :, None] == jnp.arange(held * HALF, dtype=jnp.int32)).astype(jnp.bfloat16)
    model = jnp.einsum("brs,bst->rt", routed, selector, preferred_element_type=jnp.float32)
    model = model.reshape(rows, 2, held, HALF).transpose(0, 2, 1, 3).reshape(rows, held, 2 * HALF)
    weight = jnp.cos((20.0 + band_rows.astype(jnp.float32) / 60.0) * (np.pi / 180.0))
    weight = jnp.broadcast_to(weight[:, None, None], (rows, 1, CP))

    weighted = pl.pallas_call(
        forward_kernel,
        out_shape=jax.ShapeDtypeStruct((blocks, rows * deep, CP), jnp.bfloat16),
        in_specs=[vmem] * 7,
        out_specs=vmem,
        scratch_shapes=[
            pltpu.VMEM((rows, 2 * AP, CP), jnp.float32),
            pltpu.VMEM((blocks, rows * deep, CP), jnp.float32),
        ],
        compiler_params=params,
        name="longitude_forward",
    )(h_re, h_im, model, weight, three_cols(first), twist.astype(np.float32), three_cols(second))
    columns = exchange(weighted, 1, "send_columns")

    width = deep * NA
    padded = jnp.pad(kernel, ((0, 0), (0, width * blocks - kernel.shape[1])))
    own = lax.dynamic_slice_in_dim(padded, block * width, width, 1).reshape(2 * total - 1, deep, NA)
    own = jnp.pad(own, ((0, 0), (0, 0), (0, HALF - NA)))
    own = jnp.concatenate([own, own], axis=2).astype(jnp.float32)
    summed = pl.pallas_call(
        stokes_kernel,
        out_shape=jax.ShapeDtypeStruct((blocks, rows * deep, CP), jnp.bfloat16),
        in_specs=[vmem] * 2,
        out_specs=vmem,
        scratch_shapes=[pltpu.VMEM((total, deep, CP), jnp.float32), pltpu.VMEM((total, deep, CP), jnp.float32)],
        compiler_params=params,
        name="stokes_rows",
    )(own, columns)
    returned = exchange(summed, 2, "return_sums")

    back_second = np.concatenate([second[:HALF].T, second[HALF:].T], axis=0)
    back_second = np.concatenate(numpy_pair(back_second), axis=1)
    turn = np.concatenate([twist[:, 0], twist[:, 0]], axis=1), np.concatenate([-twist[:, 1], twist[:, 1]], axis=1)
    back_twist = np.stack([turn[0].transpose(0, 2, 1), turn[1].transpose(0, 2, 1)], axis=1).astype(np.float32)
    back_first = three_cols(first.transpose(0, 2, 1))
    keep_own = jnp.where(even | (band == 1), 1.0, -1.0) * jnp.where(band == 1, -1.0, 1.0)
    keep_beside = jnp.where(lower, 1.0, -1.0)
    give_beside = jnp.where((band == 1) | (band == 2), 1.0, -1.0)
    part = rows // 2
    flat = jax.ShapeDtypeStruct((part, gravity.shape[1]), jnp.float32)
    pieces = []
    for start in range(0, rows, part):
        real, chosen = pl.pallas_call(
            functools.partial(inverse_kernel, start),
            out_shape=(flat, flat),
            in_specs=[vmem] * 4,
            out_specs=(vmem, vmem),
            scratch_shapes=[
                pltpu.VMEM((part, 2 * AP, CP), jnp.float32),
                pltpu.VMEM((blocks, part * deep, CP), jnp.float32),
            ],
            compiler_params=params,
            name="longitude_inverse",
        )(returned, back_first, back_twist, back_second)
        beside = swap((real * SHIFT).astype(jnp.float16), 1).astype(jnp.float32) / SHIFT
        give = swap(((chosen + give_beside * beside) * SHIFT).astype(jnp.float16), 2)
        pieces.append(keep_own * chosen + keep_beside * beside + give.astype(jnp.float32) / SHIFT)
    return jnp.concatenate(pieces, axis=0)


def fits(mesh):
    return mesh.shape["freq"] == 4 and HALF % mesh.shape["lat"] == 0


def solution(mesh):
    return jax.shard_map(
        band_device if fits(mesh) else general_device,
        mesh=mesh,
        in_specs=(
            P("lat", "freq"),
            P(("lat", "freq"), None, None),
            P(("lat", "freq"), None, None),
            P(),
            P("lat"),
            P(None, "freq"),
        ),
        out_specs=P("lat", "freq"),
        check_vma=False,
    )
```

```python
import jax
import jax.numpy as jnp
import numpy as np
from jax import lax
from jax.experimental import pallas as pl
from jax.experimental.pallas import tpu as pltpu
from jax.sharding import PartitionSpec as P

L = 21600
PA = 144
PB = 150
PH = 75


highest = lax.Precision.HIGHEST


def angle_table(first, second, period):
    phase = first * second % period
    return phase.astype(jnp.float32) * (2.0 * np.pi / period)


def forward_bands(grid, first_start, bands):
    rows = grid.shape[0]
    count_one = grid.shape[1]
    first_index = first_start + jnp.arange(count_one, dtype=jnp.int32)
    freq_one = jnp.arange(PA, dtype=jnp.int32)
    theta_one = angle_table(first_index[:, None], freq_one[None, :], PA)
    section_re = jnp.einsum("rab,ak->rbk", grid, jnp.cos(theta_one), precision=highest)
    section_im = -jnp.einsum("rab,ak->rbk", grid, jnp.sin(theta_one), precision=highest)
    second_index = jnp.arange(PB, dtype=jnp.int32)
    twist = angle_table(second_index[:, None], freq_one[None, :], L)
    twist_cos = jnp.cos(twist)
    twist_sin = jnp.sin(twist)
    turned_re = section_re * twist_cos + section_im * twist_sin
    turned_im = section_im * twist_cos - section_re * twist_sin
    freq_two = jnp.arange(PH, dtype=jnp.int32)
    theta_two = angle_table(second_index[:, None], freq_two[None, :], PB)
    cos_two = jnp.cos(theta_two)
    sin_two = jnp.sin(theta_two)
    spec_re = jnp.einsum("rbk,bm->rkm", turned_re, cos_two, precision=highest) + jnp.einsum(
        "rbk,bm->rkm", turned_im, sin_two, precision=highest
    )
    spec_im = jnp.einsum("rbk,bm->rkm", turned_im, cos_two, precision=highest) - jnp.einsum(
        "rbk,bm->rkm", turned_re, sin_two, precision=highest
    )
    scale = (2.0 / L) ** 0.5
    stacked = jnp.stack([spec_re, spec_im]) * scale
    span = PA // bands
    stacked = stacked.reshape(2, rows, span, bands, PH).transpose(3, 1, 0, 4, 2)
    return stacked.reshape(bands, rows, 2, PH * span)


def inverse_rows(spectra, band_ids, bands):
    count = spectra.shape[0]
    rows = spectra.shape[1]
    span = PA // bands
    parts = spectra.reshape(count, rows, 2, PH, span)
    part_re = parts[:, :, 0]
    part_im = parts[:, :, 1]
    freq_two = jnp.arange(PH, dtype=jnp.int32)
    second_index = jnp.arange(PB, dtype=jnp.int32)
    theta_two = angle_table(freq_two[:, None], second_index[None, :], PB)
    cos_two = jnp.cos(theta_two)
    sin_two = jnp.sin(theta_two)
    middle_re = jnp.einsum("brms,mn->brsn", part_re, cos_two, precision=highest) - jnp.einsum(
        "brms,mn->brsn", part_im, sin_two, precision=highest
    )
    middle_im = jnp.einsum("brms,mn->brsn", part_im, cos_two, precision=highest) + jnp.einsum(
        "brms,mn->brsn", part_re, sin_two, precision=highest
    )
    freq_one = jnp.arange(span, dtype=jnp.int32)[None, :] * bands + band_ids[:, None]
    twist = angle_table(freq_one[:, :, None], second_index[None, None, :], L)
    twist_cos = jnp.cos(twist)[:, None]
    twist_sin = jnp.sin(twist)[:, None]
    turned_re = middle_re * twist_cos - middle_im * twist_sin
    turned_im = middle_re * twist_sin + middle_im * twist_cos
    first_index = jnp.arange(PA, dtype=jnp.int32)
    theta_one = angle_table(freq_one[:, :, None], first_index[None, None, :], PA)
    grid = jnp.einsum(
        "brsn,bsa->ran", turned_re, jnp.cos(theta_one), precision=highest
    ) - jnp.einsum("brsn,bsa->ran", turned_im, jnp.sin(theta_one), precision=highest)
    return grid * (2.0 / L) ** 0.5


def general_device(gravity, coef, legendre, order_table, band_rows, kernel):
    bands = lax.axis_size("freq")
    blocks = lax.axis_size("lat")
    band_self = lax.axis_index("freq")
    block_self = lax.axis_index("lat")
    rows = gravity.shape[0]
    span = PA // bands
    local_grid = gravity.reshape(rows, span, PB)
    terms = forward_bands(local_grid, band_self * span, bands)
    observed = lax.psum_scatter(terms, "freq", scatter_dimension=0, tiled=True)[0]
    band_width = observed.shape[2]
    synth = jnp.einsum("ocn,onq->ocq", coef, legendre, preferred_element_type=jnp.float32).astype(
        jnp.bfloat16
    )
    routed = lax.all_to_all(synth, "lat", split_axis=2, concat_axis=0, tiled=True)
    per_slot = coef.shape[0]
    slot_ids = (
        (jnp.arange(blocks, dtype=jnp.int32)[:, None] * bands + band_self) * per_slot
        + jnp.arange(per_slot, dtype=jnp.int32)[None, :]
    ).reshape(-1)
    positions = order_table[slot_ids] // bands
    selector = (positions[:, None] == jnp.arange(band_width, dtype=jnp.int32)[None, :]).astype(
        jnp.bfloat16
    )
    model = jnp.einsum("jcr,jt->rct", routed, selector, preferred_element_type=jnp.float32)
    weight = jnp.cos((20.0 + band_rows.astype(jnp.float32) / 60.0) * (np.pi / 180.0))
    weighted = ((observed - model) * weight[:, None, None]).astype(jnp.bfloat16)
    total_rows = rows * blocks
    padded_width = -(-band_width // blocks) * blocks
    padding_cols = padded_width - band_width
    slab_width = padded_width // blocks
    spread = jnp.pad(weighted, ((0, 0), (0, 0), (0, padding_cols)))
    columns = lax.all_to_all(spread, "lat", split_axis=2, concat_axis=0, tiled=True)
    kernel_padded = jnp.pad(kernel, ((0, 0), (0, padding_cols)))
    kernel_own = lax.dynamic_slice_in_dim(kernel_padded, block_self * slab_width, slab_width, 1)
    full_offsets = np.arange(total_rows)[None, :] - np.arange(total_rows)[:, None] + total_rows - 1
    toeplitz_full = kernel_own[full_offsets]
    summed = jnp.einsum("pqk,qck->pck", toeplitz_full, columns, preferred_element_type=jnp.float32)
    returned = lax.all_to_all(summed, "lat", split_axis=0, concat_axis=2, tiled=True)
    stokes = returned[:, :, :band_width]
    grid_terms = inverse_rows(stokes[None], jnp.reshape(band_self, (1,)), bands)
    geoid = lax.psum_scatter(grid_terms, "freq", scatter_dimension=1, tiled=True)
    return geoid.reshape(rows, span * PB)


NA = 45
NC = 120
AP = 48
HALF = 64
CP = 128
SCALE = (2.0 / L) ** 0.5


def split_pair(values):
    high = values.astype(jnp.bfloat16)
    low = (values - high.astype(jnp.float32)).astype(jnp.bfloat16)
    return high, low


def numpy_pair(values):
    high = np.asarray(values, np.float32).astype(jnp.bfloat16)
    low = (values - high.astype(np.float64)).astype(jnp.bfloat16)
    return high, low


def tables():
    a = np.arange(NA)
    c = np.arange(NC)
    j1 = np.arange(NA)
    j2 = np.arange(NC // 2)
    first = np.zeros((4, CP, 2 * AP))
    twist = np.zeros((4, 2, HALF, CP))
    for b in range(4):
        theta = 2 * np.pi * (np.outer(4 * j1 + b, a) % (4 * NA)) / (4 * NA)
        first[b, :NA, :NA] = np.cos(theta)
        first[b, :NA, AP : AP + NA] = np.sin(theta)
        first[b, HALF : HALF + NA, :NA] = -np.sin(theta)
        first[b, HALF : HALF + NA, AP : AP + NA] = np.cos(theta)
        phi = 2 * np.pi * (np.outer(4 * j1 + b, c) % L) / L
        twist[b, 0, :NA, :NC] = np.cos(phi)
        twist[b, 1, :NA, :NC] = np.sin(phi)
    second = np.zeros((CP, CP))
    angle = 2 * np.pi * (np.outer(j2, c) % NC) / NC
    second[: NC // 2, :NC] = np.cos(angle)
    second[HALF : HALF + NC // 2, :NC] = np.sin(angle)
    return first, twist, second


def three_cols(values):
    high, low = numpy_pair(values)
    return np.concatenate([high, high, low], axis=-1)


def rows_of_three(values):
    high, low = split_pair(values)
    return jnp.concatenate([high, low, high], axis=0)


def cols_of_three(values):
    high, low = split_pair(values)
    return jnp.concatenate([high, low, high], axis=1)


def lane_sign():
    lane = lax.broadcasted_iota(jnp.int32, (1, CP), 1)
    return jnp.where(lane < HALF, 1.0, -1.0)


PIECES = ((0, 12), (12, 24), (24, 36), (36, 45))


def start_remote(src, dst, send, recv, axis, peer):
    copy = pltpu.make_async_remote_copy(
        src_ref=src,
        dst_ref=dst,
        send_sem=send,
        recv_sem=recv,
        device_id={axis: peer},
        device_id_type=pl.DeviceIdType.MESH,
    )
    copy.start()
    return copy


def residual_kernel(
    re_ref,
    im_ref,
    synth_ref,
    select_ref,
    weight_ref,
    kernel_ref,
    first_ref,
    twist_ref,
    second_ref,
    back_first_ref,
    back_twist_ref,
    back_second_ref,
    out_ref,
    grid,
    parts,
    routed,
    model,
    leaving,
    columns,
    values,
    sums,
    leaving_sums,
    returned,
    wire_one,
    wire_two,
    in_one,
    in_two,
    keep,
    near,
    route_send,
    route_recv,
    column_send,
    column_recv,
    sum_send,
    sum_recv,
    one_send,
    one_recv,
    two_send,
    two_recv,
):
    me = lax.axis_index("lat")
    band = lax.axis_index("freq")
    blocks = synth_ref.shape[0]
    rows = re_ref.shape[0]
    deep = HALF // blocks
    total = rows * blocks
    held = model.shape[1]
    peers = [lax.rem(me + d, blocks) for d in range(1, blocks)]
    beside = band + 1 - 2 * lax.rem(band, 2)
    across = lax.rem(band + 2, 4)
    barrier = pltpu.get_barrier_semaphore()
    for peer in peers:
        pl.semaphore_signal(barrier, inc=1, device_id={"lat": peer}, device_id_type=pl.DeviceIdType.MESH)
    for peer in (beside, across):
        pl.semaphore_signal(barrier, inc=1, device_id={"freq": peer}, device_id_type=pl.DeviceIdType.MESH)
    pl.semaphore_wait(barrier, blocks + 1)

    routes = [
        start_remote(synth_ref.at[peer], routed.at[me], route_send.at[d], route_recv.at[d], "lat", peer)
        for d, peer in enumerate(peers)
    ]
    own = pltpu.make_async_copy(synth_ref.at[me], routed.at[me], near)
    own.start()

    grid[...] = jnp.zeros_like(grid)
    for a in range(NA):
        grid[:, a, :NC] = re_ref[:, a * NC : (a + 1) * NC]
        grid[:, AP + a, :NC] = im_ref[:, a * NC : (a + 1) * NC]
    first = first_ref[band]
    cosine = twist_ref[band, 0]
    sine = twist_ref[band, 1]
    second = second_ref[...]
    sign = lane_sign() * SCALE
    for r in range(rows):
        section = jnp.dot(first, rows_of_three(grid[r]), preferred_element_type=jnp.float32)
        top, bottom = section[:HALF], section[HALF:]
        turned = jnp.concatenate([top * cosine + bottom * sine, bottom * cosine - top * sine], axis=0)
        both = lax.dot_general(
            second, cols_of_three(turned), (((1,), (1,)), ((), ())), preferred_element_type=jnp.float32
        )
        spectrum = both[:HALF] * SCALE + pltpu.roll(both[HALF:], HALF, 1) * sign
        parts[:, r * deep : (r + 1) * deep] = spectrum.reshape(blocks, deep, CP)

    own.wait()
    for copy in routes:
        copy.wait()
    found = jnp.zeros((2 * rows, held * HALF), jnp.float32)
    for source in range(blocks):
        found = found + jnp.dot(routed[source], select_ref[source], preferred_element_type=jnp.float32)
    for j in range(held):
        span = slice(j * HALF, (j + 1) * HALF)
        model[:, j] = jnp.concatenate([found[:rows, span], found[rows:, span]], axis=1)
    for r in range(rows):
        span = slice(r * deep, (r + 1) * deep)
        taken = model[r]
        for k in range(blocks):
            term = parts[k, span]
            if k * deep < held:
                term = term - taken[k * deep : (k + 1) * deep]
            parts[k, span] = term * weight_ref[r]
    leaving[...] = parts[...].astype(leaving.dtype)

    sent = [
        start_remote(leaving.at[peer], columns.at[me], column_send.at[d], column_recv.at[d], "lat", peer)
        for d, peer in enumerate(peers)
    ]
    own = pltpu.make_async_copy(leaving.at[me], columns.at[me], near)
    own.start()
    own.wait()
    for copy in sent:
        copy.wait()
    for source in range(blocks):
        values[source * rows : (source + 1) * rows] = columns[source].astype(jnp.float32).reshape(rows, deep, CP)

    qb = 8
    backs = []
    for d, peer in enumerate(peers + [me]):
        p0 = peer * rows

        def q_step(j, acc):
            q0 = j * qb
            base = q0 - p0 + total - rows
            window = [kernel_ref[base + e] for e in range(rows + qb - 1)]
            terms = [values[q0 + q] for q in range(qb)]
            acc = list(acc)
            for p in range(rows):
                for q in range(qb):
                    acc[p] = acc[p] + window[q - p + rows - 1] * terms[q]
            return tuple(acc)

        zero = jnp.zeros((deep, CP), jnp.float32)
        acc = lax.fori_loop(0, total // qb, q_step, (zero,) * rows)
        for p in range(rows):
            sums[p] = acc[p]
        block = sums[...].reshape(rows * deep, CP).astype(leaving_sums.dtype)
        if d < blocks - 1:
            leaving_sums[d] = block
            backs.append(
                start_remote(leaving_sums.at[d], returned.at[me], sum_send.at[d], sum_recv.at[d], "lat", peer)
            )
        else:
            returned[me] = block
    for copy in backs:
        copy.wait()

    back_first = back_first_ref[band]
    back_cosine = back_twist_ref[band, 0]
    back_sine = back_twist_ref[band, 1]
    back_second = back_second_ref[...]
    parts[...] = returned[...].astype(jnp.float32)
    for r in range(rows):
        held_sums = parts[:, r * deep : (r + 1) * deep].reshape(HALF, CP).astype(jnp.bfloat16)
        both = jnp.dot(
            back_second, jnp.concatenate([held_sums, held_sums], axis=0), preferred_element_type=jnp.float32
        )
        middle = both[:CP] * SCALE - pltpu.roll(both[CP:], HALF, 1) * sign
        turned = middle * back_cosine + pltpu.roll(middle, HALF, 1) * back_sine
        grid[r] = lax.dot_general(
            back_first, cols_of_three(turned), (((1,), (1,)), ((), ())), preferred_element_type=jnp.float32
        )

    even = 1.0 - lax.rem(band, 2).astype(jnp.float32)
    keep_own = jnp.where((band == 1) | (band == 3), -1.0, 1.0)
    keep_beside = jnp.where(band < 2, 1.0, -1.0)
    give_beside = jnp.where((band == 1) | (band == 2), 1.0, -1.0)
    ones = []
    for k, (low, high) in enumerate(PIECES):
        for a in range(low, high):
            real = grid[:, a]
            wire_one[a] = real.astype(wire_one.dtype)
            keep[a] = even * real + (1.0 - even) * grid[:, AP + a]
        piece = pl.ds(low, high - low)
        ones.append(
            start_remote(wire_one.at[piece], in_one.at[piece], one_send.at[k], one_recv.at[k], "freq", beside)
        )
    twos = []
    for k, (low, high) in enumerate(PIECES):
        ones[k].wait()
        piece = pl.ds(low, high - low)
        chosen = keep[low:high]
        arrived = in_one[low:high].astype(jnp.float32)
        wire_two[low:high] = (chosen + give_beside * arrived).astype(wire_two.dtype)
        keep[low:high] = keep_own * chosen + keep_beside * arrived
        twos.append(
            start_remote(wire_two.at[piece], in_two.at[piece], two_send.at[k], two_recv.at[k], "freq", across)
        )
    for k, (low, high) in enumerate(PIECES):
        twos[k].wait()
        for a in range(low, high):
            out_ref[:, a * NC : (a + 1) * NC] = (keep[a] + in_two[a].astype(jnp.float32))[:, :NC]


def swap(values, distance):
    return lax.ppermute(values, "freq", [(f, f ^ distance) for f in range(4)])


def band_device(gravity, coef, legendre, order_table, band_rows, kernel):
    band = lax.axis_index("freq")
    blocks = lax.axis_size("lat")
    block = lax.axis_index("lat")
    rows = gravity.shape[0]
    total = rows * blocks
    slots = coef.shape[0]
    deep = HALF // blocks
    first, twist, second = tables()
    vmem = pl.BlockSpec(memory_space=pltpu.VMEM)

    even = band % 2 == 0
    lower = band < 2
    short = gravity.astype(jnp.float16)
    across = swap(short, 2).astype(jnp.float32)
    added = gravity + across
    taken = jnp.where(lower, gravity - across, across - gravity)
    beside = swap(jnp.where(even, taken, added).astype(jnp.float16), 1).astype(jnp.float32)
    h_re = jnp.where(even, added + jnp.where(lower, beside, -beside), beside)
    h_im = jnp.where(even, 0.0, jnp.where(lower, -taken, taken))

    synth = jnp.einsum("ocn,onq->ocq", coef, legendre, preferred_element_type=jnp.float32).astype(jnp.bfloat16)
    synth = synth.reshape(slots, 2, blocks, rows).transpose(2, 1, 3, 0).reshape(blocks, 2 * rows, slots)
    synth = jnp.pad(synth, ((0, 0), (0, 0), (0, CP - slots)))
    held = -(-(-(-order_table.shape[0] // 4) // NA) // 8) * 8
    mine = lax.dynamic_index_in_dim(order_table.reshape(blocks, 4, slots), band, 1, keepdims=False)
    place = mine // 4
    lane = jnp.pad(place // NA * HALF + place % NA, ((0, 0), (0, CP - slots)), constant_values=-1)
    selector = (lane[:, :, None] == jnp.arange(held * HALF, dtype=jnp.int32)).astype(jnp.bfloat16)
    weight = jnp.cos((20.0 + band_rows.astype(jnp.float32) / 60.0) * (np.pi / 180.0))
    weight = jnp.broadcast_to(weight[:, None, None], (rows, 1, CP))

    width = deep * NA
    padded = jnp.pad(kernel, ((0, 0), (0, width * blocks - kernel.shape[1])))
    own = lax.dynamic_slice_in_dim(padded, block * width, width, 1).reshape(2 * total - 1, deep, NA)
    own = jnp.pad(own, ((0, 0), (0, 0), (0, HALF - NA)))
    own = jnp.concatenate([own, own], axis=2).astype(jnp.float32)

    back_second = np.concatenate([second[:HALF].T, second[HALF:].T], axis=0)
    back_second = np.concatenate(numpy_pair(back_second), axis=1)
    turn = np.concatenate([twist[:, 0], twist[:, 0]], axis=1), np.concatenate([-twist[:, 1], twist[:, 1]], axis=1)
    back_twist = np.stack([turn[0].transpose(0, 2, 1), turn[1].transpose(0, 2, 1)], axis=1).astype(np.float32)
    back_first = three_cols(first.transpose(0, 2, 1))

    lanes = (blocks, rows * deep, CP)
    line = (NA, rows, CP)
    wire = jnp.bfloat16
    peers = pltpu.SemaphoreType.DMA((blocks - 1,))
    pieces = pltpu.SemaphoreType.DMA((len(PIECES),))
    return pl.pallas_call(
        residual_kernel,
        out_shape=jax.ShapeDtypeStruct(gravity.shape, jnp.float32),
        in_specs=[vmem] * 12,
        out_specs=vmem,
        scratch_shapes=[
            pltpu.VMEM((rows, 2 * AP, CP), jnp.float32),
            pltpu.VMEM(lanes, jnp.float32),
            pltpu.VMEM(synth.shape, jnp.bfloat16),
            pltpu.VMEM((rows, held, CP), jnp.float32),
            pltpu.VMEM(lanes, wire),
            pltpu.VMEM(lanes, wire),
            pltpu.VMEM((total, deep, CP), jnp.float32),
            pltpu.VMEM((rows, deep, CP), jnp.float32),
            pltpu.VMEM((blocks - 1, rows * deep, CP), wire),
            pltpu.VMEM(lanes, wire),
            pltpu.VMEM(line, wire),
            pltpu.VMEM(line, wire),
            pltpu.VMEM(line, wire),
            pltpu.VMEM(line, wire),
            pltpu.VMEM(line, jnp.float32),
            pltpu.SemaphoreType.DMA,
            peers,
            peers,
            peers,
            peers,
            peers,
            peers,
            pieces,
            pieces,
            pieces,
            pieces,
        ],
        compiler_params=pltpu.CompilerParams(
            collective_id=0, has_side_effects=True, vmem_limit_bytes=48 * 2**20
        ),
        name="residual_band",
    )(
        h_re,
        h_im,
        synth,
        selector,
        weight,
        own,
        three_cols(first),
        twist.astype(np.float32),
        three_cols(second),
        back_first,
        back_twist,
        back_second,
    )


def fits(mesh):
    return mesh.shape["freq"] == 4 and HALF % mesh.shape["lat"] == 0


def solution(mesh):
    return jax.shard_map(
        band_device if fits(mesh) else general_device,
        mesh=mesh,
        in_specs=(
            P("lat", "freq"),
            P(("lat", "freq"), None, None),
            P(("lat", "freq"), None, None),
            P(),
            P("lat"),
            P(None, "freq"),
        ),
        out_specs=P("lat", "freq"),
        check_vma=False,
    )
```

```python
import jax
import jax.numpy as jnp
import numpy as np
from jax import lax
from jax.experimental import pallas as pl
from jax.experimental.pallas import tpu as pltpu
from jax.sharding import PartitionSpec as P

L = 21600
PA = 144
PB = 150
PH = 75


highest = lax.Precision.HIGHEST


def angle_table(first, second, period):
    phase = first * second % period
    return phase.astype(jnp.float32) * (2.0 * np.pi / period)


def forward_bands(grid, first_start, bands):
    rows = grid.shape[0]
    count_one = grid.shape[1]
    first_index = first_start + jnp.arange(count_one, dtype=jnp.int32)
    freq_one = jnp.arange(PA, dtype=jnp.int32)
    theta_one = angle_table(first_index[:, None], freq_one[None, :], PA)
    section_re = jnp.einsum("rab,ak->rbk", grid, jnp.cos(theta_one), precision=highest)
    section_im = -jnp.einsum("rab,ak->rbk", grid, jnp.sin(theta_one), precision=highest)
    second_index = jnp.arange(PB, dtype=jnp.int32)
    twist = angle_table(second_index[:, None], freq_one[None, :], L)
    twist_cos = jnp.cos(twist)
    twist_sin = jnp.sin(twist)
    turned_re = section_re * twist_cos + section_im * twist_sin
    turned_im = section_im * twist_cos - section_re * twist_sin
    freq_two = jnp.arange(PH, dtype=jnp.int32)
    theta_two = angle_table(second_index[:, None], freq_two[None, :], PB)
    cos_two = jnp.cos(theta_two)
    sin_two = jnp.sin(theta_two)
    spec_re = jnp.einsum("rbk,bm->rkm", turned_re, cos_two, precision=highest) + jnp.einsum(
        "rbk,bm->rkm", turned_im, sin_two, precision=highest
    )
    spec_im = jnp.einsum("rbk,bm->rkm", turned_im, cos_two, precision=highest) - jnp.einsum(
        "rbk,bm->rkm", turned_re, sin_two, precision=highest
    )
    scale = (2.0 / L) ** 0.5
    stacked = jnp.stack([spec_re, spec_im]) * scale
    span = PA // bands
    stacked = stacked.reshape(2, rows, span, bands, PH).transpose(3, 1, 0, 4, 2)
    return stacked.reshape(bands, rows, 2, PH * span)


def inverse_rows(spectra, band_ids, bands):
    count = spectra.shape[0]
    rows = spectra.shape[1]
    span = PA // bands
    parts = spectra.reshape(count, rows, 2, PH, span)
    part_re = parts[:, :, 0]
    part_im = parts[:, :, 1]
    freq_two = jnp.arange(PH, dtype=jnp.int32)
    second_index = jnp.arange(PB, dtype=jnp.int32)
    theta_two = angle_table(freq_two[:, None], second_index[None, :], PB)
    cos_two = jnp.cos(theta_two)
    sin_two = jnp.sin(theta_two)
    middle_re = jnp.einsum("brms,mn->brsn", part_re, cos_two, precision=highest) - jnp.einsum(
        "brms,mn->brsn", part_im, sin_two, precision=highest
    )
    middle_im = jnp.einsum("brms,mn->brsn", part_im, cos_two, precision=highest) + jnp.einsum(
        "brms,mn->brsn", part_re, sin_two, precision=highest
    )
    freq_one = jnp.arange(span, dtype=jnp.int32)[None, :] * bands + band_ids[:, None]
    twist = angle_table(freq_one[:, :, None], second_index[None, None, :], L)
    twist_cos = jnp.cos(twist)[:, None]
    twist_sin = jnp.sin(twist)[:, None]
    turned_re = middle_re * twist_cos - middle_im * twist_sin
    turned_im = middle_re * twist_sin + middle_im * twist_cos
    first_index = jnp.arange(PA, dtype=jnp.int32)
    theta_one = angle_table(freq_one[:, :, None], first_index[None, None, :], PA)
    grid = jnp.einsum(
        "brsn,bsa->ran", turned_re, jnp.cos(theta_one), precision=highest
    ) - jnp.einsum("brsn,bsa->ran", turned_im, jnp.sin(theta_one), precision=highest)
    return grid * (2.0 / L) ** 0.5


def general_device(gravity, coef, legendre, order_table, band_rows, kernel):
    bands = lax.axis_size("freq")
    blocks = lax.axis_size("lat")
    band_self = lax.axis_index("freq")
    block_self = lax.axis_index("lat")
    rows = gravity.shape[0]
    span = PA // bands
    local_grid = gravity.reshape(rows, span, PB)
    terms = forward_bands(local_grid, band_self * span, bands)
    observed = lax.psum_scatter(terms, "freq", scatter_dimension=0, tiled=True)[0]
    band_width = observed.shape[2]
    synth = jnp.einsum("ocn,onq->ocq", coef, legendre, preferred_element_type=jnp.float32).astype(
        jnp.bfloat16
    )
    routed = lax.all_to_all(synth, "lat", split_axis=2, concat_axis=0, tiled=True)
    per_slot = coef.shape[0]
    slot_ids = (
        (jnp.arange(blocks, dtype=jnp.int32)[:, None] * bands + band_self) * per_slot
        + jnp.arange(per_slot, dtype=jnp.int32)[None, :]
    ).reshape(-1)
    positions = order_table[slot_ids] // bands
    selector = (positions[:, None] == jnp.arange(band_width, dtype=jnp.int32)[None, :]).astype(
        jnp.bfloat16
    )
    model = jnp.einsum("jcr,jt->rct", routed, selector, preferred_element_type=jnp.float32)
    weight = jnp.cos((20.0 + band_rows.astype(jnp.float32) / 60.0) * (np.pi / 180.0))
    weighted = ((observed - model) * weight[:, None, None]).astype(jnp.bfloat16)
    total_rows = rows * blocks
    padded_width = -(-band_width // blocks) * blocks
    padding_cols = padded_width - band_width
    slab_width = padded_width // blocks
    spread = jnp.pad(weighted, ((0, 0), (0, 0), (0, padding_cols)))
    columns = lax.all_to_all(spread, "lat", split_axis=2, concat_axis=0, tiled=True)
    kernel_padded = jnp.pad(kernel, ((0, 0), (0, padding_cols)))
    kernel_own = lax.dynamic_slice_in_dim(kernel_padded, block_self * slab_width, slab_width, 1)
    full_offsets = np.arange(total_rows)[None, :] - np.arange(total_rows)[:, None] + total_rows - 1
    toeplitz_full = kernel_own[full_offsets]
    summed = jnp.einsum("pqk,qck->pck", toeplitz_full, columns, preferred_element_type=jnp.float32)
    returned = lax.all_to_all(summed, "lat", split_axis=0, concat_axis=2, tiled=True)
    stokes = returned[:, :, :band_width]
    grid_terms = inverse_rows(stokes[None], jnp.reshape(band_self, (1,)), bands)
    geoid = lax.psum_scatter(grid_terms, "freq", scatter_dimension=1, tiled=True)
    return geoid.reshape(rows, span * PB)


NA = 45
NC = 120
AP = 48
HALF = 64
CP = 128
SCALE = (2.0 / L) ** 0.5


def split_pair(values):
    high = values.astype(jnp.bfloat16)
    low = (values - high.astype(jnp.float32)).astype(jnp.bfloat16)
    return high, low


def numpy_pair(values):
    high = np.asarray(values, np.float32).astype(jnp.bfloat16)
    low = (values - high.astype(np.float64)).astype(jnp.bfloat16)
    return high, low


def tables():
    a = np.arange(NA)
    c = np.arange(NC)
    j1 = np.arange(NA)
    j2 = np.arange(NC // 2)
    first = np.zeros((4, CP, 2 * AP))
    twist = np.zeros((4, 2, HALF, CP))
    for b in range(4):
        theta = 2 * np.pi * (np.outer(4 * j1 + b, a) % (4 * NA)) / (4 * NA)
        first[b, :NA, :NA] = np.cos(theta)
        first[b, :NA, AP : AP + NA] = np.sin(theta)
        first[b, HALF : HALF + NA, :NA] = -np.sin(theta)
        first[b, HALF : HALF + NA, AP : AP + NA] = np.cos(theta)
        phi = 2 * np.pi * (np.outer(4 * j1 + b, c) % L) / L
        twist[b, 0, :NA, :NC] = np.cos(phi)
        twist[b, 1, :NA, :NC] = np.sin(phi)
    second = np.zeros((CP, CP))
    angle = 2 * np.pi * (np.outer(j2, c) % NC) / NC
    second[: NC // 2, :NC] = np.cos(angle)
    second[HALF : HALF + NC // 2, :NC] = np.sin(angle)
    return first, twist, second


def three_cols(values):
    high, low = numpy_pair(values)
    return np.concatenate([high, high, low], axis=-1)


def rows_of_three(values):
    high, low = split_pair(values)
    return jnp.concatenate([high, low, high], axis=0)


def cols_of_three(values):
    high, low = split_pair(values)
    return jnp.concatenate([high, low, high], axis=1)


def lane_sign():
    lane = lax.broadcasted_iota(jnp.int32, (1, CP), 1)
    return jnp.where(lane < HALF, 1.0, -1.0)


PIECES = 4


def start_remote(src, dst, send, recv, axis, peer):
    copy = pltpu.make_async_remote_copy(
        src_ref=src,
        dst_ref=dst,
        send_sem=send,
        recv_sem=recv,
        device_id={axis: peer},
        device_id_type=pl.DeviceIdType.MESH,
    )
    copy.start()
    return copy


def residual_kernel(
    re_ref,
    im_ref,
    synth_ref,
    select_ref,
    weight_ref,
    kernel_ref,
    first_ref,
    twist_ref,
    second_ref,
    back_first_ref,
    back_twist_ref,
    back_second_ref,
    out_ref,
    grid,
    parts,
    routing,
    routed,
    model,
    leaving,
    columns,
    values,
    window_rows,
    sums,
    leaving_sums,
    returned,
    wire_one,
    wire_two,
    in_one,
    in_two,
    near,
    route_send,
    route_recv,
    column_send,
    column_recv,
    sum_send,
    sum_recv,
    one_send,
    one_recv,
    two_send,
    two_recv,
):
    me = lax.axis_index("lat")
    band = lax.axis_index("freq")
    blocks = routing.shape[0]
    rows = re_ref.shape[0]
    deep = HALF // blocks
    total = rows * blocks
    held = model.shape[1]
    peers = [lax.rem(me + d, blocks) for d in range(1, blocks)]
    beside = band + 1 - 2 * lax.rem(band, 2)
    across = lax.rem(band + 2, 4)
    barrier = pltpu.get_barrier_semaphore()
    for peer in peers:
        pl.semaphore_signal(barrier, inc=1, device_id={"lat": peer}, device_id_type=pl.DeviceIdType.MESH)
    for peer in (beside, across):
        pl.semaphore_signal(barrier, inc=1, device_id={"freq": peer}, device_id_type=pl.DeviceIdType.MESH)
    pl.semaphore_wait(barrier, blocks + 1)

    slots = synth_ref.shape[0]
    for part in range(2):
        block = jnp.concatenate([synth_ref[:, part], jnp.zeros((CP - slots, total), jnp.float32)], axis=0).T
        routing[:, part * rows : (part + 1) * rows] = block.reshape(blocks, rows, CP).astype(routing.dtype)
    routes = [
        start_remote(routing.at[peer], routed.at[me], route_send.at[d], route_recv.at[d], "lat", peer)
        for d, peer in enumerate(peers)
    ]
    own = pltpu.make_async_copy(routing.at[me], routed.at[me], near)
    own.start()

    grid[...] = jnp.zeros_like(grid)
    for a in range(NA):
        grid[:, a, :NC] = re_ref[:, a * NC : (a + 1) * NC]
        grid[:, AP + a, :NC] = im_ref[:, a * NC : (a + 1) * NC]
    first = first_ref[band]
    cosine = twist_ref[band, 0]
    sine = twist_ref[band, 1]
    second = second_ref[...]
    sign = lane_sign() * SCALE
    for r in range(rows):
        section = jnp.dot(first, rows_of_three(grid[r]), preferred_element_type=jnp.float32)
        top, bottom = section[:HALF], section[HALF:]
        turned = jnp.concatenate([top * cosine + bottom * sine, bottom * cosine - top * sine], axis=0)
        both = lax.dot_general(
            second, cols_of_three(turned), (((1,), (1,)), ((), ())), preferred_element_type=jnp.float32
        )
        spectrum = both[:HALF] * SCALE + pltpu.roll(both[HALF:], HALF, 1) * sign
        parts[:, r * deep : (r + 1) * deep] = spectrum.reshape(blocks, deep, CP)

    own.wait()
    for copy in routes:
        copy.wait()
    found = jnp.zeros((2 * rows, held * HALF), jnp.float32)
    for source in range(blocks):
        found = found + jnp.dot(routed[source], select_ref[source], preferred_element_type=jnp.float32)
    for j in range(held):
        span = slice(j * HALF, (j + 1) * HALF)
        model[:, j] = jnp.concatenate([found[:rows, span], found[rows:, span]], axis=1)
    for r in range(rows):
        span = slice(r * deep, (r + 1) * deep)
        taken = model[r]
        for k in range(blocks):
            term = parts[k, span]
            if k * deep < held:
                term = term - taken[k * deep : (k + 1) * deep]
            parts[k, span] = term * weight_ref[r]
    leaving[...] = parts[...].astype(leaving.dtype)

    sent = [
        start_remote(leaving.at[peer], columns.at[me], column_send.at[d], column_recv.at[d], "lat", peer)
        for d, peer in enumerate(peers)
    ]
    own = pltpu.make_async_copy(leaving.at[me], columns.at[me], near)
    own.start()
    gap = jnp.zeros((kernel_ref.shape[0], HALF - NA), jnp.float32)
    for j in range(deep):
        piece = kernel_ref[:, j * NA : (j + 1) * NA]
        window_rows[:, j] = jnp.concatenate([piece, gap, piece, gap], axis=1)
    own.wait()
    for copy in sent:
        copy.wait()
    for source in range(blocks):
        values[source * rows : (source + 1) * rows] = columns[source].astype(jnp.float32).reshape(rows, deep, CP)

    qb = 8
    backs = []
    for d, peer in enumerate(peers + [me]):
        p0 = peer * rows

        def q_step(j, acc):
            q0 = j * qb
            base = q0 - p0 + total - rows
            window = [window_rows[base + e] for e in range(rows + qb - 1)]
            terms = [values[q0 + q] for q in range(qb)]
            acc = list(acc)
            for p in range(rows):
                for q in range(qb):
                    acc[p] = acc[p] + window[q - p + rows - 1] * terms[q]
            return tuple(acc)

        zero = jnp.zeros((deep, CP), jnp.float32)
        acc = lax.fori_loop(0, total // qb, q_step, (zero,) * rows)
        for p in range(rows):
            sums[p] = acc[p]
        block = sums[...].reshape(rows * deep, CP).astype(leaving_sums.dtype)
        if d < blocks - 1:
            leaving_sums[d] = block
            backs.append(
                start_remote(leaving_sums.at[d], returned.at[me], sum_send.at[d], sum_recv.at[d], "lat", peer)
            )
        else:
            returned[me] = block
    for copy in backs:
        copy.wait()

    back_first = back_first_ref[band]
    back_cosine = back_twist_ref[band, 0]
    back_sine = back_twist_ref[band, 1]
    back_second = back_second_ref[...]
    parts[...] = returned[...].astype(jnp.float32)
    even = 1.0 - lax.rem(band, 2).astype(jnp.float32)
    keep_own = jnp.where((band == 1) | (band == 3), -1.0, 1.0)
    keep_beside = jnp.where(band < 2, 1.0, -1.0)
    give_beside = jnp.where((band == 1) | (band == 2), 1.0, -1.0)
    step = rows // PIECES
    ones = []
    for r in range(rows):
        held_sums = parts[:, r * deep : (r + 1) * deep].reshape(HALF, CP).astype(jnp.bfloat16)
        both = jnp.dot(
            back_second, jnp.concatenate([held_sums, held_sums], axis=0), preferred_element_type=jnp.float32
        )
        middle = both[:CP] * SCALE - pltpu.roll(both[CP:], HALF, 1) * sign
        turned = middle * back_cosine + pltpu.roll(middle, HALF, 1) * back_sine
        both = lax.dot_general(
            back_first, cols_of_three(turned), (((1,), (1,)), ((), ())), preferred_element_type=jnp.float32
        )
        real = both[:AP]
        wire_one[r] = real.astype(wire_one.dtype)
        grid[r, :AP] = even * real + (1.0 - even) * both[AP:]
        if (r + 1) % step == 0:
            k = r // step
            piece = pl.ds(k * step, step)
            ones.append(
                start_remote(wire_one.at[piece], in_one.at[piece], one_send.at[k], one_recv.at[k], "freq", beside)
            )
    twos = []
    for k in range(PIECES):
        ones[k].wait()
        piece = pl.ds(k * step, step)
        chosen = grid[piece, :AP]
        arrived = in_one[piece].astype(jnp.float32)
        wire_two[piece] = (chosen + give_beside * arrived).astype(wire_two.dtype)
        grid[piece, :AP] = keep_own * chosen + keep_beside * arrived
        twos.append(
            start_remote(wire_two.at[piece], in_two.at[piece], two_send.at[k], two_recv.at[k], "freq", across)
        )
    for k in range(PIECES):
        twos[k].wait()
        piece = pl.ds(k * step, step)
        grid[piece, :AP] = grid[piece, :AP] + in_two[piece].astype(jnp.float32)
    for a in range(NA):
        out_ref[:, a * NC : (a + 1) * NC] = grid[:, a, :NC]


def swap(values, distance):
    return lax.ppermute(values, "freq", [(f, f ^ distance) for f in range(4)])


def band_device(gravity, coef, legendre, order_table, band_rows, kernel):
    band = lax.axis_index("freq")
    blocks = lax.axis_size("lat")
    block = lax.axis_index("lat")
    rows = gravity.shape[0]
    total = rows * blocks
    slots = coef.shape[0]
    deep = HALF // blocks
    first, twist, second = tables()
    vmem = pl.BlockSpec(memory_space=pltpu.VMEM)

    even = band % 2 == 0
    lower = band < 2
    short = gravity.astype(jnp.float16)
    across = swap(short, 2).astype(jnp.float32)
    added = gravity + across
    taken = jnp.where(lower, gravity - across, across - gravity)
    cut = slots // 2
    lead = jnp.einsum("ocn,onq->ocq", coef[:cut], legendre[:cut], preferred_element_type=jnp.float32)
    given = jnp.where(even, taken, added).astype(jnp.float16)
    given, rest, lead = lax.optimization_barrier((given, coef[cut:], lead))
    beside = swap(given, 1).astype(jnp.float32)
    tail = jnp.einsum("ocn,onq->ocq", rest, legendre[cut:], preferred_element_type=jnp.float32)
    synth = jnp.concatenate([lead, tail], axis=0)
    h_re = jnp.where(even, added + jnp.where(lower, beside, -beside), beside)
    h_im = jnp.where(even, 0.0, jnp.where(lower, -taken, taken))

    held = -(-(-(-order_table.shape[0] // 4) // NA) // 8) * 8
    mine = lax.dynamic_index_in_dim(order_table.reshape(blocks, 4, slots), band, 1, keepdims=False)
    place = mine // 4
    lane = jnp.pad(place // NA * HALF + place % NA, ((0, 0), (0, CP - slots)), constant_values=-1)
    selector = (lane[:, :, None] == jnp.arange(held * HALF, dtype=jnp.int32)).astype(jnp.bfloat16)
    weight = jnp.cos((20.0 + band_rows.astype(jnp.float32) / 60.0) * (np.pi / 180.0))
    weight = jnp.broadcast_to(weight[:, None, None], (rows, 1, CP))

    width = deep * NA
    padded = jnp.pad(kernel, ((0, 0), (0, width * blocks - kernel.shape[1])))
    own = lax.dynamic_slice_in_dim(padded, block * width, width, 1).astype(jnp.float32)

    back_second = np.concatenate([second[:HALF].T, second[HALF:].T], axis=0)
    back_second = np.concatenate(numpy_pair(back_second), axis=1)
    turn = np.concatenate([twist[:, 0], twist[:, 0]], axis=1), np.concatenate([-twist[:, 1], twist[:, 1]], axis=1)
    back_twist = np.stack([turn[0].transpose(0, 2, 1), turn[1].transpose(0, 2, 1)], axis=1).astype(np.float32)
    back_first = three_cols(first.transpose(0, 2, 1))

    lanes = (blocks, rows * deep, CP)
    line = (rows, AP, CP)
    wire = jnp.bfloat16
    peers = pltpu.SemaphoreType.DMA((blocks - 1,))
    pieces = pltpu.SemaphoreType.DMA((PIECES,))
    return pl.pallas_call(
        residual_kernel,
        out_shape=jax.ShapeDtypeStruct(gravity.shape, jnp.float32),
        in_specs=[vmem] * 12,
        out_specs=vmem,
        scratch_shapes=[
            pltpu.VMEM((rows, 2 * AP, CP), jnp.float32),
            pltpu.VMEM(lanes, jnp.float32),
            pltpu.VMEM((blocks, 2 * rows, CP), jnp.bfloat16),
            pltpu.VMEM((blocks, 2 * rows, CP), jnp.bfloat16),
            pltpu.VMEM((rows, held, CP), jnp.float32),
            pltpu.VMEM(lanes, wire),
            pltpu.VMEM(lanes, wire),
            pltpu.VMEM((total, deep, CP), jnp.float32),
            pltpu.VMEM((2 * total - 1, deep, CP), jnp.float32),
            pltpu.VMEM((rows, deep, CP), jnp.float32),
            pltpu.VMEM((blocks - 1, rows * deep, CP), wire),
            pltpu.VMEM(lanes, wire),
            pltpu.VMEM(line, wire),
            pltpu.VMEM(line, wire),
            pltpu.VMEM(line, wire),
            pltpu.VMEM(line, wire),
            pltpu.SemaphoreType.DMA,
            peers,
            peers,
            peers,
            peers,
            peers,
            peers,
            pieces,
            pieces,
            pieces,
            pieces,
        ],
        compiler_params=pltpu.CompilerParams(
            collective_id=0, has_side_effects=True, vmem_limit_bytes=48 * 2**20
        ),
        name="residual_band",
    )(
        h_re,
        h_im,
        synth,
        selector,
        weight,
        own,
        three_cols(first),
        twist.astype(np.float32),
        three_cols(second),
        back_first,
        back_twist,
        back_second,
    )


def fits(mesh):
    return mesh.shape["freq"] == 4 and HALF % mesh.shape["lat"] == 0


def solution(mesh):
    return jax.shard_map(
        band_device if fits(mesh) else general_device,
        mesh=mesh,
        in_specs=(
            P("lat", "freq"),
            P(("lat", "freq"), None, None),
            P(("lat", "freq"), None, None),
            P(),
            P("lat"),
            P(None, "freq"),
        ),
        out_specs=P("lat", "freq"),
        check_vma=False,
    )
```

```python
import jax
import jax.numpy as jnp
import numpy as np
from jax import lax
from jax.experimental import pallas as pl
from jax.experimental.pallas import tpu as pltpu
from jax.sharding import PartitionSpec as P

L = 21600
PA = 144
PB = 150
PH = 75


highest = lax.Precision.HIGHEST


def angle_table(first, second, period):
    phase = first * second % period
    return phase.astype(jnp.float32) * (2.0 * np.pi / period)


def forward_bands(grid, first_start, bands):
    rows = grid.shape[0]
    count_one = grid.shape[1]
    first_index = first_start + jnp.arange(count_one, dtype=jnp.int32)
    freq_one = jnp.arange(PA, dtype=jnp.int32)
    theta_one = angle_table(first_index[:, None], freq_one[None, :], PA)
    section_re = jnp.einsum("rab,ak->rbk", grid, jnp.cos(theta_one), precision=highest)
    section_im = -jnp.einsum("rab,ak->rbk", grid, jnp.sin(theta_one), precision=highest)
    second_index = jnp.arange(PB, dtype=jnp.int32)
    twist = angle_table(second_index[:, None], freq_one[None, :], L)
    twist_cos = jnp.cos(twist)
    twist_sin = jnp.sin(twist)
    turned_re = section_re * twist_cos + section_im * twist_sin
    turned_im = section_im * twist_cos - section_re * twist_sin
    freq_two = jnp.arange(PH, dtype=jnp.int32)
    theta_two = angle_table(second_index[:, None], freq_two[None, :], PB)
    cos_two = jnp.cos(theta_two)
    sin_two = jnp.sin(theta_two)
    spec_re = jnp.einsum("rbk,bm->rkm", turned_re, cos_two, precision=highest) + jnp.einsum(
        "rbk,bm->rkm", turned_im, sin_two, precision=highest
    )
    spec_im = jnp.einsum("rbk,bm->rkm", turned_im, cos_two, precision=highest) - jnp.einsum(
        "rbk,bm->rkm", turned_re, sin_two, precision=highest
    )
    scale = (2.0 / L) ** 0.5
    stacked = jnp.stack([spec_re, spec_im]) * scale
    span = PA // bands
    stacked = stacked.reshape(2, rows, span, bands, PH).transpose(3, 1, 0, 4, 2)
    return stacked.reshape(bands, rows, 2, PH * span)


def inverse_rows(spectra, band_ids, bands):
    count = spectra.shape[0]
    rows = spectra.shape[1]
    span = PA // bands
    parts = spectra.reshape(count, rows, 2, PH, span)
    part_re = parts[:, :, 0]
    part_im = parts[:, :, 1]
    freq_two = jnp.arange(PH, dtype=jnp.int32)
    second_index = jnp.arange(PB, dtype=jnp.int32)
    theta_two = angle_table(freq_two[:, None], second_index[None, :], PB)
    cos_two = jnp.cos(theta_two)
    sin_two = jnp.sin(theta_two)
    middle_re = jnp.einsum("brms,mn->brsn", part_re, cos_two, precision=highest) - jnp.einsum(
        "brms,mn->brsn", part_im, sin_two, precision=highest
    )
    middle_im = jnp.einsum("brms,mn->brsn", part_im, cos_two, precision=highest) + jnp.einsum(
        "brms,mn->brsn", part_re, sin_two, precision=highest
    )
    freq_one = jnp.arange(span, dtype=jnp.int32)[None, :] * bands + band_ids[:, None]
    twist = angle_table(freq_one[:, :, None], second_index[None, None, :], L)
    twist_cos = jnp.cos(twist)[:, None]
    twist_sin = jnp.sin(twist)[:, None]
    turned_re = middle_re * twist_cos - middle_im * twist_sin
    turned_im = middle_re * twist_sin + middle_im * twist_cos
    first_index = jnp.arange(PA, dtype=jnp.int32)
    theta_one = angle_table(freq_one[:, :, None], first_index[None, None, :], PA)
    grid = jnp.einsum(
        "brsn,bsa->ran", turned_re, jnp.cos(theta_one), precision=highest
    ) - jnp.einsum("brsn,bsa->ran", turned_im, jnp.sin(theta_one), precision=highest)
    return grid * (2.0 / L) ** 0.5


def general_device(gravity, coef, legendre, order_table, band_rows, kernel):
    bands = lax.axis_size("freq")
    blocks = lax.axis_size("lat")
    band_self = lax.axis_index("freq")
    block_self = lax.axis_index("lat")
    rows = gravity.shape[0]
    span = PA // bands
    local_grid = gravity.reshape(rows, span, PB)
    terms = forward_bands(local_grid, band_self * span, bands)
    observed = lax.psum_scatter(terms, "freq", scatter_dimension=0, tiled=True)[0]
    band_width = observed.shape[2]
    synth = jnp.einsum("ocn,onq->ocq", coef, legendre, preferred_element_type=jnp.float32).astype(
        jnp.bfloat16
    )
    routed = lax.all_to_all(synth, "lat", split_axis=2, concat_axis=0, tiled=True)
    per_slot = coef.shape[0]
    slot_ids = (
        (jnp.arange(blocks, dtype=jnp.int32)[:, None] * bands + band_self) * per_slot
        + jnp.arange(per_slot, dtype=jnp.int32)[None, :]
    ).reshape(-1)
    positions = order_table[slot_ids] // bands
    selector = (positions[:, None] == jnp.arange(band_width, dtype=jnp.int32)[None, :]).astype(
        jnp.bfloat16
    )
    model = jnp.einsum("jcr,jt->rct", routed, selector, preferred_element_type=jnp.float32)
    weight = jnp.cos((20.0 + band_rows.astype(jnp.float32) / 60.0) * (np.pi / 180.0))
    weighted = ((observed - model) * weight[:, None, None]).astype(jnp.bfloat16)
    total_rows = rows * blocks
    padded_width = -(-band_width // blocks) * blocks
    padding_cols = padded_width - band_width
    slab_width = padded_width // blocks
    spread = jnp.pad(weighted, ((0, 0), (0, 0), (0, padding_cols)))
    columns = lax.all_to_all(spread, "lat", split_axis=2, concat_axis=0, tiled=True)
    kernel_padded = jnp.pad(kernel, ((0, 0), (0, padding_cols)))
    kernel_own = lax.dynamic_slice_in_dim(kernel_padded, block_self * slab_width, slab_width, 1)
    full_offsets = np.arange(total_rows)[None, :] - np.arange(total_rows)[:, None] + total_rows - 1
    toeplitz_full = kernel_own[full_offsets]
    summed = jnp.einsum("pqk,qck->pck", toeplitz_full, columns, preferred_element_type=jnp.float32)
    returned = lax.all_to_all(summed, "lat", split_axis=0, concat_axis=2, tiled=True)
    stokes = returned[:, :, :band_width]
    grid_terms = inverse_rows(stokes[None], jnp.reshape(band_self, (1,)), bands)
    geoid = lax.psum_scatter(grid_terms, "freq", scatter_dimension=1, tiled=True)
    return geoid.reshape(rows, span * PB)


NA = 45
NC = 120
AP = 48
HALF = 64
CP = 128
SCALE = (2.0 / L) ** 0.5


def split_pair(values):
    high = values.astype(jnp.bfloat16)
    low = (values - high.astype(jnp.float32)).astype(jnp.bfloat16)
    return high, low


def numpy_pair(values):
    high = np.asarray(values, np.float32).astype(jnp.bfloat16)
    low = (values - high.astype(np.float64)).astype(jnp.bfloat16)
    return high, low


def tables():
    a = np.arange(NA)
    c = np.arange(NC)
    j1 = np.arange(NA)
    j2 = np.arange(NC // 2)
    first = np.zeros((4, CP, 2 * AP))
    twist = np.zeros((4, 2, HALF, CP))
    for b in range(4):
        theta = 2 * np.pi * (np.outer(4 * j1 + b, a) % (4 * NA)) / (4 * NA)
        first[b, :NA, :NA] = np.cos(theta)
        first[b, :NA, AP : AP + NA] = np.sin(theta)
        first[b, HALF : HALF + NA, :NA] = -np.sin(theta)
        first[b, HALF : HALF + NA, AP : AP + NA] = np.cos(theta)
        phi = 2 * np.pi * (np.outer(4 * j1 + b, c) % L) / L
        twist[b, 0, :NA, :NC] = np.cos(phi)
        twist[b, 1, :NA, :NC] = np.sin(phi)
    second = np.zeros((CP, CP))
    angle = 2 * np.pi * (np.outer(j2, c) % NC) / NC
    second[: NC // 2, :NC] = np.cos(angle)
    second[HALF : HALF + NC // 2, :NC] = np.sin(angle)
    return first, twist, second


def three_cols(values):
    high, low = numpy_pair(values)
    return np.concatenate([high, high, low], axis=-1)


def rows_of_three(values):
    high, low = split_pair(values)
    return jnp.concatenate([high, low, high], axis=0)


def cols_of_three(values):
    high, low = split_pair(values)
    return jnp.concatenate([high, low, high], axis=1)


def lane_sign():
    lane = lax.broadcasted_iota(jnp.int32, (1, CP), 1)
    return jnp.where(lane < HALF, 1.0, -1.0)


PIECES = 4


def start_remote(src, dst, send, recv, axis, peer):
    copy = pltpu.make_async_remote_copy(
        src_ref=src,
        dst_ref=dst,
        send_sem=send,
        recv_sem=recv,
        device_id={axis: peer},
        device_id_type=pl.DeviceIdType.MESH,
    )
    copy.start()
    return copy


def residual_kernel(
    re_ref,
    im_ref,
    synth_ref,
    select_ref,
    weight_ref,
    kernel_ref,
    first_ref,
    twist_ref,
    second_ref,
    back_first_ref,
    back_twist_ref,
    back_second_ref,
    out_ref,
    grid,
    parts,
    routing,
    routed,
    model,
    leaving,
    columns,
    values,
    window_rows,
    sums,
    leaving_sums,
    returned,
    wire_one,
    wire_two,
    in_one,
    in_two,
    near,
    route_send,
    route_recv,
    column_send,
    column_recv,
    sum_send,
    sum_recv,
    one_send,
    one_recv,
    two_send,
    two_recv,
):
    me = lax.axis_index("lat")
    band = lax.axis_index("freq")
    blocks = routing.shape[0]
    rows = re_ref.shape[0]
    deep = HALF // blocks
    total = rows * blocks
    held = model.shape[1]
    peers = [lax.rem(me + d, blocks) for d in range(1, blocks)]
    beside = band + 1 - 2 * lax.rem(band, 2)
    across = lax.rem(band + 2, 4)
    barrier = pltpu.get_barrier_semaphore()
    for peer in peers:
        pl.semaphore_signal(barrier, inc=1, device_id={"lat": peer}, device_id_type=pl.DeviceIdType.MESH)
    for peer in (beside, across):
        pl.semaphore_signal(barrier, inc=1, device_id={"freq": peer}, device_id_type=pl.DeviceIdType.MESH)
    pl.semaphore_wait(barrier, blocks + 1)

    slots = synth_ref.shape[0]
    for part in range(2):
        block = jnp.concatenate([synth_ref[:, part], jnp.zeros((CP - slots, total), jnp.float32)], axis=0).T
        routing[:, part * rows : (part + 1) * rows] = block.reshape(blocks, rows, CP).astype(routing.dtype)
    routes = [
        start_remote(routing.at[peer], routed.at[me], route_send.at[d], route_recv.at[d], "lat", peer)
        for d, peer in enumerate(peers)
    ]
    own = pltpu.make_async_copy(routing.at[me], routed.at[me], near)
    own.start()

    grid[...] = jnp.zeros_like(grid)
    for a in range(NA):
        grid[:, a, :NC] = re_ref[:, a * NC : (a + 1) * NC]
        grid[:, AP + a, :NC] = im_ref[:, a * NC : (a + 1) * NC]
    first = first_ref[band]
    cosine = twist_ref[band, 0]
    sine = twist_ref[band, 1]
    second = second_ref[...]
    sign = lane_sign() * SCALE
    for r in range(rows):
        section = jnp.dot(first, rows_of_three(grid[r]), preferred_element_type=jnp.float32)
        top, bottom = section[:HALF], section[HALF:]
        turned = jnp.concatenate([top * cosine + bottom * sine, bottom * cosine - top * sine], axis=0)
        both = lax.dot_general(
            second, cols_of_three(turned), (((1,), (1,)), ((), ())), preferred_element_type=jnp.float32
        )
        spectrum = both[:HALF] * SCALE + pltpu.roll(both[HALF:], HALF, 1) * sign
        parts[:, r * deep : (r + 1) * deep] = spectrum.reshape(blocks, deep, CP)

    own.wait()
    for copy in routes:
        copy.wait()
    found = jnp.zeros((2 * rows, held * HALF), jnp.float32)
    for source in range(blocks):
        found = found + jnp.dot(routed[source], select_ref[source], preferred_element_type=jnp.float32)
    for j in range(held):
        span = slice(j * HALF, (j + 1) * HALF)
        model[:, j] = jnp.concatenate([found[:rows, span], found[rows:, span]], axis=1)
    for r in range(rows):
        span = slice(r * deep, (r + 1) * deep)
        taken = model[r]
        for k in range(blocks):
            term = parts[k, span]
            if k * deep < held:
                term = term - taken[k * deep : (k + 1) * deep]
            parts[k, span] = term * weight_ref[r]
    leaving[...] = parts[...].astype(leaving.dtype)

    sent = [
        start_remote(leaving.at[peer], columns.at[me], column_send.at[d], column_recv.at[d], "lat", peer)
        for d, peer in enumerate(peers)
    ]
    own = pltpu.make_async_copy(leaving.at[me], columns.at[me], near)
    own.start()
    gap = jnp.zeros((kernel_ref.shape[0], HALF - NA), jnp.float32)
    for j in range(deep):
        piece = kernel_ref[:, j * NA : (j + 1) * NA]
        window_rows[:, j] = jnp.concatenate([piece, gap, piece, gap], axis=1)
    own.wait()
    for copy in sent:
        copy.wait()
    for source in range(blocks):
        values[source * rows : (source + 1) * rows] = columns[source].astype(jnp.float32).reshape(rows, deep, CP)

    qb = 8
    backs = []
    for d, peer in enumerate(peers + [me]):
        p0 = peer * rows

        def q_step(j, acc):
            q0 = j * qb
            base = q0 - p0 + total - rows
            window = [window_rows[base + e] for e in range(rows + qb - 1)]
            terms = [values[q0 + q] for q in range(qb)]
            acc = list(acc)
            for p in range(rows):
                for q in range(qb):
                    acc[p] = acc[p] + window[q - p + rows - 1] * terms[q]
            return tuple(acc)

        zero = jnp.zeros((deep, CP), jnp.float32)
        acc = lax.fori_loop(0, total // qb, q_step, (zero,) * rows)
        for p in range(rows):
            sums[p] = acc[p]
        block = sums[...].reshape(rows * deep, CP).astype(leaving_sums.dtype)
        if d < blocks - 1:
            leaving_sums[d] = block
            backs.append(
                start_remote(leaving_sums.at[d], returned.at[me], sum_send.at[d], sum_recv.at[d], "lat", peer)
            )
        else:
            returned[me] = block
    for copy in backs:
        copy.wait()

    back_first = back_first_ref[band]
    back_cosine = back_twist_ref[band, 0]
    back_sine = back_twist_ref[band, 1]
    back_second = back_second_ref[...]
    parts[...] = returned[...].astype(jnp.float32)
    even = 1.0 - lax.rem(band, 2).astype(jnp.float32)
    keep_own = jnp.where((band == 1) | (band == 3), -1.0, 1.0)
    keep_beside = jnp.where(band < 2, 1.0, -1.0)
    give_beside = jnp.where((band == 1) | (band == 2), 1.0, -1.0)
    step = rows // PIECES
    ones = []
    for r in range(rows):
        held_sums = parts[:, r * deep : (r + 1) * deep].reshape(HALF, CP).astype(jnp.bfloat16)
        both = jnp.dot(
            back_second, jnp.concatenate([held_sums, held_sums], axis=0), preferred_element_type=jnp.float32
        )
        middle = both[:CP] * SCALE - pltpu.roll(both[CP:], HALF, 1) * sign
        turned = middle * back_cosine + pltpu.roll(middle, HALF, 1) * back_sine
        both = lax.dot_general(
            back_first, cols_of_three(turned), (((1,), (1,)), ((), ())), preferred_element_type=jnp.float32
        )
        real = both[:AP]
        wire_one[r] = real.astype(wire_one.dtype)
        grid[r, :AP] = even * real + (1.0 - even) * both[AP:]
        if (r + 1) % step == 0:
            k = r // step
            piece = pl.ds(k * step, step)
            ones.append(
                start_remote(wire_one.at[piece], in_one.at[piece], one_send.at[k], one_recv.at[k], "freq", beside)
            )
    twos = []
    for k in range(PIECES):
        ones[k].wait()
        piece = pl.ds(k * step, step)
        chosen = grid[piece, :AP]
        arrived = in_one[piece].astype(jnp.float32)
        wire_two[piece] = (chosen + give_beside * arrived).astype(wire_two.dtype)
        grid[piece, :AP] = keep_own * chosen + keep_beside * arrived
        twos.append(
            start_remote(wire_two.at[piece], in_two.at[piece], two_send.at[k], two_recv.at[k], "freq", across)
        )
    for k in range(PIECES):
        twos[k].wait()
        piece = pl.ds(k * step, step)
        grid[piece, :AP] = grid[piece, :AP] + in_two[piece].astype(jnp.float32)
    for a in range(NA):
        out_ref[:, a * NC : (a + 1) * NC] = grid[:, a, :NC]


def synthesis_kernel(coef_ref, legendre_ref, out_ref):
    for k in range(out_ref.shape[0]):
        out_ref[k] = jnp.dot(coef_ref[k], legendre_ref[k], preferred_element_type=jnp.float32)


def synthesis(coef, legendre, start, count):
    _, degrees, rows = legendre.shape
    step = 4
    return pl.pallas_call(
        synthesis_kernel,
        grid=(count // step,),
        out_shape=jax.ShapeDtypeStruct((count, 2, rows), jnp.float32),
        in_specs=[
            pl.BlockSpec((step, 2, degrees), lambda i: (i + start // step, 0, 0)),
            pl.BlockSpec((step, degrees, rows), lambda i: (i + start // step, 0, 0)),
        ],
        out_specs=pl.BlockSpec((step, 2, rows), lambda i: (i, 0, 0)),
        compiler_params=pltpu.CompilerParams(vmem_limit_bytes=24 * 2**20),
        cost_estimate=pl.CostEstimate(
            flops=4 * count * degrees * rows, bytes_accessed=2 * count * degrees * (rows + 2), transcendentals=0
        ),
        name="synthesis",
    )(coef, legendre)


def swap(values, distance):
    return lax.ppermute(values, "freq", [(f, f ^ distance) for f in range(4)])


def band_device(gravity, coef, legendre, order_table, band_rows, kernel):
    band = lax.axis_index("freq")
    blocks = lax.axis_size("lat")
    block = lax.axis_index("lat")
    rows = gravity.shape[0]
    total = rows * blocks
    slots = coef.shape[0]
    deep = HALF // blocks
    first, twist, second = tables()
    vmem = pl.BlockSpec(memory_space=pltpu.VMEM)

    even = band % 2 == 0
    lower = band < 2
    short = gravity.astype(jnp.float16)
    across = swap(short, 2).astype(jnp.float32)
    added = gravity + across
    taken = jnp.where(lower, gravity - across, across - gravity)
    cut = slots // 8 * 4 + 4
    lead = synthesis(coef, legendre, 0, cut)
    given = jnp.where(even, taken, added).astype(jnp.float16)
    given, rest, lead = lax.optimization_barrier((given, coef, lead))
    beside = swap(given, 1).astype(jnp.float32)
    tail = synthesis(rest, legendre, cut, slots - cut)
    synth = jnp.concatenate([lead, tail], axis=0)
    h_re = jnp.where(even, added + jnp.where(lower, beside, -beside), beside)
    h_im = jnp.where(even, 0.0, jnp.where(lower, -taken, taken))

    held = -(-(-(-order_table.shape[0] // 4) // NA) // 8) * 8
    mine = lax.dynamic_index_in_dim(order_table.reshape(blocks, 4, slots), band, 1, keepdims=False)
    place = mine // 4
    lane = jnp.pad(place // NA * HALF + place % NA, ((0, 0), (0, CP - slots)), constant_values=-1)
    selector = (lane[:, :, None] == jnp.arange(held * HALF, dtype=jnp.int32)).astype(jnp.bfloat16)
    weight = jnp.cos((20.0 + band_rows.astype(jnp.float32) / 60.0) * (np.pi / 180.0))
    weight = jnp.broadcast_to(weight[:, None, None], (rows, 1, CP))

    width = deep * NA
    padded = jnp.pad(kernel, ((0, 0), (0, width * blocks - kernel.shape[1])))
    own = lax.dynamic_slice_in_dim(padded, block * width, width, 1).astype(jnp.float32)

    back_second = np.concatenate([second[:HALF].T, second[HALF:].T], axis=0)
    back_second = np.concatenate(numpy_pair(back_second), axis=1)
    turn = np.concatenate([twist[:, 0], twist[:, 0]], axis=1), np.concatenate([-twist[:, 1], twist[:, 1]], axis=1)
    back_twist = np.stack([turn[0].transpose(0, 2, 1), turn[1].transpose(0, 2, 1)], axis=1).astype(np.float32)
    back_first = three_cols(first.transpose(0, 2, 1))

    lanes = (blocks, rows * deep, CP)
    line = (rows, AP, CP)
    wire = jnp.bfloat16
    peers = pltpu.SemaphoreType.DMA((blocks - 1,))
    pieces = pltpu.SemaphoreType.DMA((PIECES,))
    return pl.pallas_call(
        residual_kernel,
        out_shape=jax.ShapeDtypeStruct(gravity.shape, jnp.float32),
        in_specs=[vmem] * 12,
        out_specs=vmem,
        scratch_shapes=[
            pltpu.VMEM((rows, 2 * AP, CP), jnp.float32),
            pltpu.VMEM(lanes, jnp.float32),
            pltpu.VMEM((blocks, 2 * rows, CP), jnp.bfloat16),
            pltpu.VMEM((blocks, 2 * rows, CP), jnp.bfloat16),
            pltpu.VMEM((rows, held, CP), jnp.float32),
            pltpu.VMEM(lanes, wire),
            pltpu.VMEM(lanes, wire),
            pltpu.VMEM((total, deep, CP), jnp.float32),
            pltpu.VMEM((2 * total - 1, deep, CP), jnp.float32),
            pltpu.VMEM((rows, deep, CP), jnp.float32),
            pltpu.VMEM((blocks - 1, rows * deep, CP), wire),
            pltpu.VMEM(lanes, wire),
            pltpu.VMEM(line, wire),
            pltpu.VMEM(line, wire),
            pltpu.VMEM(line, wire),
            pltpu.VMEM(line, wire),
            pltpu.SemaphoreType.DMA,
            peers,
            peers,
            peers,
            peers,
            peers,
            peers,
            pieces,
            pieces,
            pieces,
            pieces,
        ],
        compiler_params=pltpu.CompilerParams(
            collective_id=0, has_side_effects=True, vmem_limit_bytes=48 * 2**20
        ),
        name="residual_band",
    )(
        h_re,
        h_im,
        synth,
        selector,
        weight,
        own,
        three_cols(first),
        twist.astype(np.float32),
        three_cols(second),
        back_first,
        back_twist,
        back_second,
    )


def fits(mesh):
    return mesh.shape["freq"] == 4 and HALF % mesh.shape["lat"] == 0 and mesh.shape["lat"] == 8


def solution(mesh):
    return jax.shard_map(
        band_device if fits(mesh) else general_device,
        mesh=mesh,
        in_specs=(
            P("lat", "freq"),
            P(("lat", "freq"), None, None),
            P(("lat", "freq"), None, None),
            P(),
            P("lat"),
            P(None, "freq"),
        ),
        out_specs=P("lat", "freq"),
        check_vma=False,
    )
```
